256 devices in a mesh: pipe: 4 (over y_lo, core), expert: 64 (over x, z, y_hi).
Axes of the slice: x: 4, y: 4 (y_hi: 2, y_lo: 2; y = y_hi * 2 + y_lo), z: 8, core: 2. Of those that a mesh axis runs over, the one named last changes fastest.
Arguments:
- tokens: bfloat16 [32768, 3584], P(('pipe', 'expert')), may hold values from -6 to 6
- expert_ids: int32 [32768, 8], P(('pipe', 'expert')), may hold values from 0 to 255, all different within a row; in each aligned block of 128 rows (0 to 127, 128 to 255, ...) at most 8 rows name the same one
- gate_values: bfloat16 [32768, 8], P(('pipe', 'expert')), may hold values from 0.25 to 2.5
- cotangent: bfloat16 [32768, 3584], P(('pipe', 'expert')), may hold values from -0.1796875 to 0.1796875
- w_gate: bfloat16 [3584, 16384], P(None, 'expert'), may hold values from -0.09375 to 0.09375
- w_up: bfloat16 [3584, 16384], P(None, 'expert'), may hold values from -0.09375 to 0.09375
- w_down: bfloat16 [16384, 3584], P('expert'), may hold values from -0.125 to 0.125
Outputs:
- mixed: bfloat16 [32768, 3584], P(('pipe', 'expert'))
- gate_grad: float32 [32768, 8], P(('pipe', 'expert'))
- grad_gate: bfloat16 [4, 3584, 16384], P('pipe', None, 'expert')
- grad_up: bfloat16 [4, 3584, 16384], P('pipe', None, 'expert')
The draws below stay inside these ranges and needn't reach their ends.
Inputs may be any that keep to these rules, and one draw needn't show every extreme that they name: `expert_ids`: each row names 8 different experts; within the rows of one device no expert is named by more than 8 rows, a bound that some block reaches.
All inputs are finite; a program needn't handle non-finite values.
Results may differ from the reference program's by a relative error of at most 0.02.
Values may be sent and summed in bfloat16 or wider, within the bound.
A program may use at most 128 MiB of HBM per device.

```python
import math
import jax
import jax.numpy as jnp
import numpy as np

D = 3584
FFW = 2048
ROUTED = 256
TOPK = 8
SLICES = 8
TOK_DEV = 128
CAP = 8
HIDALL = 16384
TOKENS = 32768
N_PIPE = 4
N_EXPERT = 64


def block_scale(key, shape, shards, smallest, high):
    factor_of = 1.0
    for dim, blocks in shards:
        draws = jax.random.uniform(jax.random.fold_in(jax.random.fold_in(key, 6), dim), (blocks,), jnp.float32, smallest / len(shards), high / len(shards))
        factor_of = factor_of * jnp.repeat(jnp.exp(draws), shape[dim] // blocks).reshape((-1,) + (1,) * (len(shape) - 1 - dim))
    return factor_of


def deal_out(key, own, number, rows, number_of, top, reach, slope):
    ranking = jax.random.permutation(key, number_of)
    crowded, ordinary = portions_of(number_of, rows * top, reach, slope, True), portions_of(number_of, rows * top, reach, slope, False)
    places = jnp.arange(number_of)

    def named(tallies, turn):
        used = int((tallies > 0).sum())
        fixed = max(1, used // 4)
        moved = fixed + (places - fixed + turn * (used - fixed)) % max(1, number_of - fixed)
        return jnp.zeros((number_of,), jnp.int32).at[ranking[jnp.where(places < fixed, places, moved)]].set(jnp.asarray(tallies, jnp.int32))

    tallies = jnp.where(number % 4 == 0, named(crowded, number // 4), named(ordinary, number - number // 4 - 1))
    mixed = jax.random.permutation(jax.random.fold_in(own, 3), number_of)
    donor, receiver = mixed[0:number_of // 2 * 2:2], mixed[1:number_of // 2 * 2:2]
    slack = jnp.minimum(tallies[donor] - 1, reach - tallies[receiver]) // 2
    slack = jnp.where((donor == ranking[0]) | (receiver == ranking[0]) | (tallies[receiver] == 0), 0, jnp.maximum(slack, 0))
    moved = jax.random.randint(jax.random.fold_in(own, 4), (number_of // 2,), 0, 1 << 20) % (slack + 1)
    tallies = tallies.at[donor].add(-moved).at[receiver].add(moved)
    items = jnp.searchsorted(jnp.cumsum(tallies), jnp.arange(rows * top), side="right").astype(jnp.int32)
    table = items.reshape(top, rows).T
    table = table[jax.random.permutation(jax.random.fold_in(own, 1), rows)]
    turn = jax.random.randint(jax.random.fold_in(own, 2), (rows, 1), 0, top)
    return jnp.take_along_axis(table, (jnp.arange(top)[None, :] + turn) % top, axis=1)


def portions_of(amount, total, limit, lean, full):
    weights = [(1 << 20) // math.isqrt(rank ** lean) + 1 for rank in range(1, amount + 1)]
    largest = limit if full else min(limit, max(-(-total // amount), total * weights[0] // sum(weights)))
    least = 1 if total - largest >= amount - 1 else 0
    given, spare = [largest] + [least] * (amount - 1), total - largest - least * (amount - 1)
    while spare > 0:
        free = [i for i in range(1, amount) if given[i] < largest] or [i for i in range(1, amount) if given[i] < limit]
        pool, left = sum([weights[i] for i in free]), spare
        for i in free:
            addition = min(limit - given[i], max(1, left * weights[i] // pool), spare)
            given[i] = given[i] + addition
            spare = spare - addition
    return np.array(given)


def noise(own_key, dims, scale, limit, shards=(), kind=jnp.bfloat16):
    entries = jax.random.normal(own_key, dims, jnp.float32) * scale
    if len(shards) > 0:
        entries = block_scale(own_key, dims, shards, -0.22, 0.18) * entries
    return jnp.clip(entries, min=-limit, max=limit).astype(kind)


def setup_inputs(seed: int = 0) -> dict:
    arg_keys = jax.random.split(jax.random.key(seed), 8)
    tokens = noise(arg_keys[0], (TOKENS, D), 1.0, 6.0, ((0, 256),))
    expert_ids_keys = jax.random.split(jax.random.fold_in(arg_keys[1], 1), TOKENS // TOK_DEV)
    expert_ids_turns = jax.random.permutation(jax.random.fold_in(arg_keys[1], 3), TOKENS // TOK_DEV)
    expert_ids = jax.vmap(lambda own, number: deal_out(jax.random.fold_in(arg_keys[1], 2), own, number, TOK_DEV, ROUTED, TOPK, CAP, 2))(expert_ids_keys, expert_ids_turns).reshape((TOKENS, TOPK))
    gate_values = jnp.clip(0.25 + 2.25 * jax.random.uniform(arg_keys[2], (TOKENS, TOPK), jnp.float32) ** block_scale(arg_keys[2], (TOKENS, TOPK), ((0, 256),), -0.2, 0.2), 0.25, 2.5).astype(jnp.bfloat16)
    cotangent = noise(arg_keys[3], (TOKENS, D), 0.03, 0.1796875, ((0, 256),))
    w_gate = noise(arg_keys[4], (D, HIDALL), D ** -0.5, 0.09375, ((1, 64),))
    w_up = noise(arg_keys[5], (D, HIDALL), D ** -0.5, 0.09375, ((1, 64),))
    w_down = noise(arg_keys[6], (HIDALL, D), FFW ** -0.5, 0.125, ((0, 64),))
    return {"tokens": tokens, "expert_ids": expert_ids, "gate_values": gate_values, "cotangent": cotangent, "w_gate": w_gate, "w_up": w_up, "w_down": w_down}


def slot_tables(expert_ids, gate_values, flight_count, capacity):
    experts = jnp.arange(flight_count, dtype=jnp.int32)
    match = (expert_ids[:, :, None] == experts[None, None, :]).astype(jnp.float32)
    counted = jnp.sum(match, axis=1)
    before = jnp.cumsum(counted, axis=0) - counted
    places = jnp.arange(capacity, dtype=jnp.float32)
    slot_hit = counted[:, :, None] * (before[:, :, None] == places[None, None, :]).astype(jnp.float32)
    gate_each = jnp.sum(match * gate_values.astype(jnp.float32)[:, :, None], axis=1)
    return match, slot_hit, gate_each


def dispatch_device(expert_ids, gate_values, token_rows, cot_rows, flight_count, capacity):
    match, slot_hit, gate_each = slot_tables(expert_ids, gate_values, flight_count, capacity)
    token_buf = jnp.einsum('tec,td->ecd', slot_hit, token_rows.astype(jnp.float32)).astype(jnp.bfloat16)
    cot_buf = jnp.einsum('tec,td->ecd', slot_hit, cot_rows.astype(jnp.float32)).astype(jnp.bfloat16)
    gate_buf = jnp.einsum('tec,te->ec', slot_hit, gate_each).astype(jnp.bfloat16)
    return token_buf, cot_buf, gate_buf, match, slot_hit, gate_each


def gate_gradient(match, slot_hit, values):
    value_each = jnp.einsum('tec,ec->te', slot_hit, values)
    return jnp.einsum('tke,te->tk', match, value_each)


def combine_device(slot_hit, gate_each, summed):
    return jnp.einsum('tec,te,ecd->td', slot_hit, gate_each, summed).astype(jnp.bfloat16)


def reference(tokens, expert_ids, gate_values, cotangent, w_gate, w_up, w_down):
    hidden_dev = FFW // SLICES
    flight_count = N_EXPERT // SLICES
    token_all = tokens.reshape(N_PIPE, N_EXPERT, TOK_DEV, D)
    ids_all = expert_ids.reshape(N_PIPE, N_EXPERT, TOK_DEV, TOPK)
    gates_all = gate_values.reshape(N_PIPE, N_EXPERT, TOK_DEV, TOPK)
    cot_all = cotangent.reshape(N_PIPE, N_EXPERT, TOK_DEV, D)
    terms_gate, terms_up, gate_grads, mixed_all = [], [], [], []
    for section_rank in range(N_PIPE):
        token_buf, cot_buf, gate_buf, match, slot_hit, gate_each = jax.vmap(
            dispatch_device, in_axes=(0, 0, 0, 0, None, None))(
            ids_all[section_rank], gates_all[section_rank], token_all[section_rank], cot_all[section_rank],
            flight_count, CAP)
        blocks_gate, blocks_up, values, sums = [], [], [], []
        for group in range(flight_count):
            token_rows = token_buf[:, group].reshape(N_EXPERT * CAP, D)
            cot_rows = cot_buf[:, group].reshape(N_EXPERT * CAP, D)
            gate_rows = gate_buf[:, group].reshape(N_EXPERT * CAP)
            start = group * FFW
            weight_gate = w_gate[:, start:start + FFW]
            weight_up = w_up[:, start:start + FFW]
            weight_down = w_down[start:start + FFW]
            pre_gate = jnp.dot(token_rows, weight_gate, preferred_element_type=jnp.float32)
            pre_up = jnp.dot(token_rows, weight_up, preferred_element_type=jnp.float32)
            sigmoid_gate = jax.nn.sigmoid(pre_gate)
            hidden = (pre_gate * sigmoid_gate * pre_up).astype(jnp.bfloat16)
            parts = jnp.einsum('rsh,shd->srd',
                               hidden.reshape(N_EXPERT * CAP, SLICES, hidden_dev).astype(jnp.float32),
                               weight_down.reshape(SLICES, hidden_dev, D).astype(jnp.float32)).astype(jnp.bfloat16)
            parts_wide = parts.astype(jnp.float32)
            sums.append(jnp.sum(parts_wide, axis=0).reshape(N_EXPERT, CAP, D))
            score = jnp.einsum('srd,rd->r', parts_wide, cot_rows.astype(jnp.float32))
            values.append(score.reshape(N_EXPERT, CAP))
            scaled = (gate_rows.astype(jnp.float32)[:, None] * cot_rows.astype(jnp.float32)).astype(jnp.bfloat16)
            back_hidden = jnp.dot(scaled, weight_down.T, preferred_element_type=jnp.float32)
            d_up = (back_hidden * pre_gate * sigmoid_gate).astype(jnp.bfloat16)
            d_pre = (back_hidden * pre_up * sigmoid_gate * (1.0 + pre_gate * (1.0 - sigmoid_gate))).astype(jnp.bfloat16)
            blocks_gate.append(jnp.dot(token_rows.T, d_pre, preferred_element_type=jnp.float32))
            blocks_up.append(jnp.dot(token_rows.T, d_up, preferred_element_type=jnp.float32))
        values = jnp.stack(values, axis=1)
        summed = jnp.stack(sums, axis=1)
        mixed_all.append(jax.vmap(combine_device)(slot_hit, gate_each, summed))
        gate_grads.append(jax.vmap(gate_gradient)(match, slot_hit, values))
        terms_gate.append(jnp.concatenate(blocks_gate, axis=1).astype(jnp.bfloat16))
        terms_up.append(jnp.concatenate(blocks_up, axis=1).astype(jnp.bfloat16))
    grad_gate = jnp.stack([(terms_gate[rank].astype(jnp.float32) + terms_gate[N_PIPE - 1 - rank].astype(jnp.float32)).astype(jnp.bfloat16) for rank in range(N_PIPE)])
    grad_up = jnp.stack([(terms_up[rank].astype(jnp.float32) + terms_up[N_PIPE - 1 - rank].astype(jnp.float32)).astype(jnp.bfloat16) for rank in range(N_PIPE)])
    gate_grad = jnp.stack(gate_grads).reshape(TOKENS, TOPK)
    mixed = jnp.stack(mixed_all).reshape(TOKENS, D)
    return mixed, gate_grad, grad_gate, grad_up
```

```python
import jax
import jax.numpy as jnp
from jax import lax
from jax.experimental import pallas as pl
from jax.experimental.pallas import tpu as pltpu
from jax.sharding import PartitionSpec as P

FFW = 2048
CAP = 8
MESH = pl.DeviceIdType.MESH
NX, NZ, NY = 4, 8, 4
PLANE = NX * NZ
GRP = 4
NG = PLANE // GRP


def where_am_i():
    p, i = lax.axis_index("pipe"), lax.axis_index("expert")
    x, z, y_hi = i // (2 * NZ), (i // 2) % NZ, i % 2
    return p, x, 2 * y_hi + p // 2, z, p % 2


def device_at(x, y, z, core):
    return ((y % 2) * 2 + core, (x * NZ + z) * 2 + y // 2)


def offset_of(k):
    return k // NZ, k % NZ


def ahead(x, z, k):
    dx, dz = offset_of(k)
    return (x + dx) % NX, (z + dz) % NZ


def behind(x, z, k):
    dx, dz = offset_of(k)
    return (x + NX - dx) % NX, (z + NZ - dz) % NZ


def greet_plane(barrier, x, y, z, core):
    def greet(k, carry):
        xd, zd = ahead(x, z, k)
        pl.semaphore_signal(
            barrier, inc=1, device_id=device_at(xd, y, zd, core), device_id_type=MESH
        )
        return carry

    lax.fori_loop(1, PLANE, greet, 0)


def dispatch_kernel(
    send_x, send_c, out_x, out_c, stage, plane_send, plane_recv, y_send, y_recv
):
    p, x, y, z, core = where_am_i()
    up, down, across = (y + 1) % NY, (y + NY - 1) % NY, (y + 2) % NY
    barrier = pltpu.get_barrier_semaphore()
    greet_plane(barrier, x, y, z, core)

    @pl.when(core == 0)
    def _():
        pl.semaphore_signal(
            barrier, inc=1, device_id=device_at(x, across, z, core), device_id_type=MESH
        )
        pl.semaphore_wait(barrier, PLANE)

    @pl.when(core == 1)
    def _():
        for to in (up, down):
            pl.semaphore_signal(
                barrier, inc=1, device_id=device_at(x, to, z, core), device_id_type=MESH
            )
        pl.semaphore_wait(barrier, PLANE + 1)

    sends = (send_x, send_c)
    outs = (out_x, out_c)

    def plane_copy(a, k):
        xd, zd = ahead(x, z, k)
        return pltpu.make_async_remote_copy(
            src_ref=sends[a].at[xd * 2 + zd // 4],
            dst_ref=stage.at[a, k],
            send_sem=plane_send.at[a, k],
            recv_sem=plane_recv.at[a, k],
            device_id=device_at(xd, y, zd, core),
            device_id_type=MESH,
        )

    def own_copy(a):
        return pltpu.make_async_copy(
            sends[a].at[x * 2 + z // 4], stage.at[a, 0], plane_recv.at[a, 0]
        )

    def y_copy(a, g, half, to):
        rows = pl.ds(g * GRP, GRP)
        return pltpu.make_async_remote_copy(
            src_ref=stage.at[a, rows],
            dst_ref=outs[a].at[pl.ds(half * PLANE + g * GRP, GRP)],
            send_sem=y_send.at[a, half, g],
            recv_sem=y_recv.at[a, half, g],
            device_id=device_at(x, to, z, core),
            device_id_type=MESH,
        )

    def keep_copy(a, g):
        rows = pl.ds(g * GRP, GRP)
        return pltpu.make_async_copy(stage.at[a, rows], outs[a].at[rows], y_recv.at[a, 0, g])

    for a in range(2):
        own_copy(a).start()

        def start(k, carry, a=a):
            plane_copy(a, k).start()
            return carry

        lax.fori_loop(1, PLANE, start, 0)

    for a in range(2):
        own_copy(a).wait()

        def forward(g, carry, a=a):
            def arrived(k, inner):
                plane_copy(a, k).wait_recv()
                return inner

            lax.fori_loop(jnp.maximum(g * GRP, 1), g * GRP + GRP, arrived, 0)

            @pl.when(core == 0)
            def _():
                y_copy(a, g, 1, across).start()
                keep_copy(a, g).start()

            @pl.when(core == 1)
            def _():
                y_copy(a, g, 0, up).start()
                y_copy(a, g, 1, down).start()

            return carry

        lax.fori_loop(0, NG, forward, 0)

    for a in range(2):

        def finish_plane(k, carry, a=a):
            plane_copy(a, k).wait_send()
            return carry

        lax.fori_loop(1, PLANE, finish_plane, 0)

        def finish(g, carry, a=a):
            @pl.when(core == 0)
            def _():
                y_copy(a, g, 1, across).wait()
                keep_copy(a, g).wait()

            @pl.when(core == 1)
            def _():
                y_copy(a, g, 0, up).wait()
                y_copy(a, g, 1, down).wait()

            return carry

        lax.fori_loop(0, NG, finish, 0)


def return_kernel(
    part,
    terms,
    out_rows,
    out_gate,
    out_up,
    landed,
    summed,
    theirs,
    total,
    plane_send,
    plane_recv,
    y_send,
    y_recv,
    core_send,
    core_recv,
    sum_send,
    sum_recv,
    keep_sem,
):
    p, x, y, z, core = where_am_i()
    up, down, across = (y + 1) % NY, (y + NY - 1) % NY, (y + 2) % NY
    partner = y + 1 - 2 * (y % 2)
    half_rows = terms.shape[0] // 2
    barrier = pltpu.get_barrier_semaphore()
    greet_plane(barrier, x, y, z, core)

    def greet(to_y, to_core):
        pl.semaphore_signal(
            barrier, inc=1, device_id=device_at(x, to_y, z, to_core), device_id_type=MESH
        )

    @pl.when(core == 0)
    def _():
        greet(across, 0)
        greet(y, 1)

    @pl.when(core == 1)
    def _():
        greet(up, 1)
        greet(down, 1)
        greet(y, 0)
        greet(partner, 0)

    pl.semaphore_wait(barrier, PLANE + 2)

    def y_copy(g, half, to):
        return pltpu.make_async_remote_copy(
            src_ref=part.at[pl.ds(half * PLANE + g * GRP, GRP)],
            dst_ref=landed.at[half, pl.ds(g * GRP, GRP)],
            send_sem=y_send.at[half, g],
            recv_sem=y_recv.at[half, g],
            device_id=device_at(x, to, z, core),
            device_id_type=MESH,
        )

    def plane_copy(k):
        xd, zd = behind(x, z, k)
        return pltpu.make_async_remote_copy(
            src_ref=summed.at[k],
            dst_ref=out_rows.at[x * NZ + z],
            send_sem=plane_send.at[k],
            recv_sem=plane_recv.at[k],
            device_id=device_at(xd, y, zd, core),
            device_id_type=MESH,
        )

    def own_copy():
        return pltpu.make_async_copy(summed.at[0], out_rows.at[x * NZ + z], plane_recv.at[0])

    def core_copy():
        other = (1 - core) * half_rows
        return pltpu.make_async_remote_copy(
            src_ref=terms.at[pl.ds(other, half_rows)],
            dst_ref=theirs,
            send_sem=core_send,
            recv_sem=core_recv,
            device_id=device_at(x, y, z, 1 - core),
            device_id_type=MESH,
        )

    outs = (out_gate, out_up)

    def sum_copy(w, half, to_y, to_core):
        return pltpu.make_async_remote_copy(
            src_ref=total.at[w],
            dst_ref=outs[w].at[pl.ds(half * half_rows, half_rows)],
            send_sem=sum_send.at[w, to_core],
            recv_sem=sum_recv.at[w, half],
            device_id=device_at(x, to_y, z, to_core),
            device_id_type=MESH,
        )

    def keep_copy(w):
        return pltpu.make_async_copy(
            total.at[w], outs[w].at[pl.ds(0, half_rows)], keep_sem.at[w]
        )

    core_copy().start()

    def start_y(g, carry):
        @pl.when(core == 0)
        def _():
            y_copy(g, 1, across).start()

        @pl.when(core == 1)
        def _():
            y_copy(g, 0, down).start()
            y_copy(g, 1, up).start()

        return carry

    lax.fori_loop(0, NG, start_y, 0)

    core_copy().wait()
    step = 16
    columns = total.shape[-1]

    def add_terms(t, carry):
        at = pl.ds(t * step, step)
        mine = terms[pl.ds(core * half_rows + t * step, step)].astype(jnp.float32)
        both = (mine + theirs[at].astype(jnp.float32)).astype(jnp.bfloat16)
        total[0, at] = both[:, :, :columns]
        total[1, at] = both[:, :, columns:]
        return carry

    lax.fori_loop(0, half_rows // step, add_terms, 0)

    @pl.when(core == 0)
    def _():
        for w in range(2):
            sum_copy(w, 0, partner, 1).start()
            keep_copy(w).start()

    @pl.when(core == 1)
    def _():
        for w in range(2):
            sum_copy(w, 1, partner, 1).start()
            sum_copy(w, 1, y, 0).start()

    def add_and_send(g, carry):
        @pl.when(core == 0)
        def _():
            y_copy(g, 1, across).wait()

            def add(b, inner):
                summed[b] = (
                    part[b].astype(jnp.float32) + landed[1, b].astype(jnp.float32)
                ).astype(jnp.bfloat16)
                return inner

            lax.fori_loop(g * GRP, g * GRP + GRP, add, 0)

        @pl.when(core == 1)
        def _():
            y_copy(g, 0, down).wait()
            y_copy(g, 1, up).wait()

            def add(b, inner):
                summed[b] = (
                    landed[0, b].astype(jnp.float32) + landed[1, b].astype(jnp.float32)
                ).astype(jnp.bfloat16)
                return inner

            lax.fori_loop(g * GRP, g * GRP + GRP, add, 0)

        def send(k, inner):
            plane_copy(k).start()
            return inner

        lax.fori_loop(jnp.maximum(g * GRP, 1), g * GRP + GRP, send, 0)
        return carry

    lax.fori_loop(0, NG, add_and_send, 0)
    own_copy().start()
    own_copy().wait()

    def finish(k, carry):
        plane_copy(k).wait()
        return carry

    lax.fori_loop(1, PLANE, finish, 0)

    @pl.when(core == 0)
    def _():
        for w in range(2):
            sum_copy(w, 0, partner, 1).wait_send()
            keep_copy(w).wait()
            sum_copy(w, 1, y, 0).wait_recv()

    @pl.when(core == 1)
    def _():
        for w in range(2):
            sum_copy(w, 1, partner, 1).wait()
            sum_copy(w, 1, y, 0).wait_send()
            sum_copy(w, 0, partner, 1).wait_recv()


def dispatch(send_x, send_c):
    block = send_x.shape[1:]
    landed = jax.ShapeDtypeStruct((2 * PLANE,) + block, jnp.bfloat16)
    return pl.pallas_call(
        dispatch_kernel,
        out_shape=(landed, landed),
        in_specs=[pl.BlockSpec(memory_space=pltpu.VMEM)] * 2,
        out_specs=[pl.BlockSpec(memory_space=pl.ANY)] * 2,
        scratch_shapes=[
            pltpu.VMEM((2, PLANE) + block, jnp.bfloat16),
            pltpu.SemaphoreType.DMA((2, PLANE)),
            pltpu.SemaphoreType.DMA((2, PLANE)),
            pltpu.SemaphoreType.DMA((2, 2, NG)),
            pltpu.SemaphoreType.DMA((2, 2, NG)),
        ],
        compiler_params=pltpu.CompilerParams(
            collective_id=0, has_side_effects=True, vmem_limit_bytes=24 << 20
        ),
    )(send_x, send_c)


def give_back(part, terms):
    block = part.shape[1:]
    blocks, rows, columns = terms.shape
    grad = jax.ShapeDtypeStruct((blocks, rows, columns // 2), jnp.bfloat16)
    dma = pltpu.SemaphoreType.DMA
    return pl.pallas_call(
        return_kernel,
        out_shape=(jax.ShapeDtypeStruct((PLANE,) + block, jnp.bfloat16), grad, grad),
        in_specs=[pl.BlockSpec(memory_space=pltpu.VMEM)] * 2,
        out_specs=[pl.BlockSpec(memory_space=pl.ANY)] * 3,
        scratch_shapes=[
            pltpu.VMEM((2, PLANE) + block, jnp.bfloat16),
            pltpu.VMEM((PLANE,) + block, jnp.bfloat16),
            pltpu.VMEM((blocks // 2, rows, columns), jnp.bfloat16),
            pltpu.VMEM((2, blocks // 2, rows, columns // 2), jnp.bfloat16),
            dma((PLANE,)),
            dma((PLANE,)),
            dma((2, NG)),
            dma((2, NG)),
            dma,
            dma,
            dma((2, 2)),
            dma((2, 2)),
            dma((2,)),
        ],
        compiler_params=pltpu.CompilerParams(
            collective_id=1, has_side_effects=True, vmem_limit_bytes=40 << 20
        ),
    )(part, terms)


def slot_tables(expert_ids, gate_values, flight_count, capacity):
    experts = jnp.arange(flight_count, dtype=jnp.int32)
    match = (expert_ids[:, :, None] == experts[None, None, :]).astype(jnp.float32)
    counted = jnp.sum(match, axis=1)
    before = jnp.cumsum(counted, axis=0) - counted
    places = jnp.arange(capacity, dtype=jnp.float32)
    slot_hit = counted[:, :, None] * (before[:, :, None] == places[None, None, :]).astype(
        jnp.float32
    )
    gate_each = jnp.sum(match * gate_values.astype(jnp.float32)[:, :, None], axis=1)
    return (match, slot_hit, gate_each)


def per_device(tokens, expert_ids, gate_values, cotangent, w_gate, w_up, w_down):
    device_count = lax.axis_size("expert")
    hidden_dev = w_gate.shape[1]
    slice_count = FFW // hidden_dev
    flight_count = device_count // slice_count
    width = tokens.shape[1]
    capacity = CAP
    f32, bf16 = jnp.float32, jnp.bfloat16
    row_contract = (((0,), (0,)), ((), ()))
    match, slot_hit, gate_each = slot_tables(expert_ids, gate_values, flight_count, capacity)
    hit_flat = slot_hit.reshape(slot_hit.shape[0], flight_count * capacity).astype(bf16)
    token_buf = lax.dot_general(hit_flat, tokens, row_contract, preferred_element_type=f32)
    cot_buf = lax.dot_general(hit_flat, cotangent, row_contract, preferred_element_type=f32)
    gate_buf = jnp.sum(slot_hit * gate_each[:, :, None], axis=0).reshape(-1, 1)

    def to_blocks(rows):
        return rows.astype(bf16).reshape(flight_count, capacity, width)

    recv_x, recv_c = dispatch(to_blocks(token_buf), to_blocks(gate_buf * cot_buf))
    token_rows, scaled = recv_x.reshape(-1, width), recv_c.reshape(-1, width)
    pre_gate = jnp.dot(token_rows, w_gate, preferred_element_type=f32)
    pre_up = jnp.dot(token_rows, w_up, preferred_element_type=f32)
    sigmoid_gate = jax.nn.sigmoid(pre_gate)
    hidden = (pre_gate * sigmoid_gate * pre_up).astype(bf16)
    partial_out = jnp.dot(hidden, w_down, preferred_element_type=f32).astype(bf16)
    partial_out = partial_out.reshape(device_count, capacity, width)
    back_hidden = lax.dot_general(
        scaled, w_down, (((1,), (1,)), ((), ())), preferred_element_type=f32
    )
    d_up = (back_hidden * pre_gate * sigmoid_gate).astype(bf16)
    d_pre = (back_hidden * pre_up * sigmoid_gate * (1.0 + pre_gate * (1.0 - sigmoid_gate))).astype(
        bf16
    )
    terms = lax.dot_general(
        token_rows,
        jnp.concatenate([d_pre, d_up], axis=1),
        row_contract,
        preferred_element_type=f32,
    ).astype(bf16)
    returned, grad_gate, grad_up = give_back(partial_out, terms.reshape(-1, capacity, 2 * hidden_dev))

    copies = PLANE // flight_count
    weight_hit = (slot_hit * gate_each[:, :, None]).astype(bf16)
    weight_hit = jnp.repeat(weight_hit, copies, axis=1).reshape(tokens.shape[0], -1)
    mixed = jnp.dot(
        weight_hit, returned.reshape(-1, width), preferred_element_type=f32
    ).astype(bf16)
    returned = returned.reshape(flight_count, copies, capacity, width).astype(f32)
    cots = cot_buf.reshape(flight_count, 1, capacity, width)
    values = jnp.sum(returned * cots, axis=(1, 3))
    value_each = jnp.einsum("tec,ec->te", slot_hit, values, precision=lax.Precision.HIGHEST)
    gate_grad = jnp.einsum("tke,te->tk", match, value_each, precision=lax.Precision.HIGHEST)
    grad_shape = (1, width, hidden_dev)
    return (mixed, gate_grad, grad_gate.reshape(grad_shape), grad_up.reshape(grad_shape))


def solution(mesh):
    placed = (
        P(("pipe", "expert"), None),
        P(("pipe", "expert"), None),
        P(("pipe", "expert"), None),
        P(("pipe", "expert"), None),
        P(None, "expert"),
        P(None, "expert"),
        P("expert", None),
    )
    return jax.shard_map(
        per_device,
        mesh=mesh,
        in_specs=placed,
        out_specs=(
            P(("pipe", "expert"), None),
            P(("pipe", "expert"), None),
            P("pipe", None, "expert"),
            P("pipe", None, "expert"),
        ),
        check_vma=False,
    )
```

```python
import jax
import jax.numpy as jnp
from jax import lax
from jax.experimental import pallas as pl
from jax.experimental.pallas import tpu as pltpu
from jax.sharding import PartitionSpec as P

FFW = 2048
CAP = 8
MESH = pl.DeviceIdType.MESH
NX, NZ, NY = 4, 8, 4
PLANE = NX * NZ
PAIRS = NZ // 2
HALF = NX * PAIRS
GRP = 4
NG = PLANE // GRP
CHUNKS = 4
TILE = 256


def where_am_i():
    p, i = lax.axis_index("pipe"), lax.axis_index("expert")
    x, z, y_hi = i // (2 * NZ), (i // 2) % NZ, i % 2
    return p, x, 2 * y_hi + p // 2, z, p % 2


def device_at(x, y, z, core):
    return ((y % 2) * 2 + core, (x * NZ + z) * 2 + y // 2)


def source_of(x, z, k):
    sign = 1 - 2 * (z % 2)
    far, dx, t = k // HALF, k // PAIRS % NX, k % PAIRS
    dz = far * (t + 1) - (1 - far) * t
    return (x + NX - dx) % NX, (z + NZ + sign * dz) % NZ


def relay_of(x, z, k):
    sign = 1 - 2 * (z % 2)
    dx, t = k // PAIRS, k % PAIRS
    dz = t * (1 - 2 * (t % 2))
    return (x + dx) % NX, (z + NZ + sign * dz) % NZ


def rank_kernel(
    send_x,
    send_c,
    w_gate,
    w_up,
    w_down,
    out_rows,
    out_gate,
    out_up,
    stage,
    x_land,
    x_rows,
    c_mid,
    c_land,
    w_land,
    w_rows,
    pre,
    hidden,
    back,
    grad,
    slopes,
    parts,
    parts_in,
    sums,
    mine,
    theirs,
    total,
    x_relay,
    x_pair,
    x_y,
    c_y,
    c_relay,
    c_pair,
    w_sem,
    h_sem,
    b_sem,
    p_sem,
    s_sem,
    core_sem,
    t_sem,
):
    p, x, y, z, core = where_am_i()
    up, down, across = (y + 1) % NY, (y + NY - 1) % NY, (y + 2) % NY
    partner, beside = y + 1 - 2 * (y % 2), (y + NY - 1 + 2 * (y % 2)) % NY
    pair = z + 1 - 2 * (z % 2)
    y_hi = y // 2
    f32, bf16 = jnp.float32, jnp.bfloat16
    slots, _, rows_each, width = x_land.shape
    half = width // 2
    hid = w_gate.shape[1]
    chunk_slots = slots // CHUNKS
    chunk = chunk_slots * 2 * rows_each
    tiles = theirs.shape[0]

    def copy_to(src, dst, sems, at, to):
        return pltpu.make_async_remote_copy(
            src_ref=src,
            dst_ref=dst,
            send_sem=sems.at[(0,) + at[0]],
            recv_sem=sems.at[(1,) + at[1]],
            device_id=device_at(*to),
            device_id_type=MESH,
        )

    def loop(first, last, body):
        def step(i, carry):
            body(i)
            return carry

        lax.fori_loop(first, last, step, 0)

    barrier = pltpu.get_barrier_semaphore()

    def greet(xd, yd, zd, to_core):
        pl.semaphore_signal(
            barrier, inc=1, device_id=device_at(xd, yd, zd, to_core), device_id_type=MESH
        )

    def greet_source(k):
        xs, zs = source_of(x, z, k)
        greet(xs, y, zs, core)

    loop(1, PLANE, greet_source)
    greet(x, across, z, core)
    greet(x, y, z, 1 - core)

    @pl.when(core == 0)
    def _():
        greet(x, beside, z, 0)

    @pl.when(core == 1)
    def _():
        greet(x, up, z, 1)
        greet(x, down, z, 1)
        greet(x, partner, z, 0)

    pl.semaphore_wait(barrier, PLANE + 3)

    def x_relay_copy(k):
        xd, zd = relay_of(x, z, k)
        src = send_x.at[xd * 2 + zd // 4]
        return copy_to(src, stage.at[k], x_relay, ((k,), (k,)), (xd, y, zd, core))

    def x_own_copy():
        return pltpu.make_async_copy(send_x.at[x * 2 + z // 4], stage.at[0], x_relay.at[1, 0])

    def x_pair_copy(g):
        src = stage.at[pl.ds(g * GRP, GRP)]
        dst = stage.at[pl.ds(HALF + g * GRP, GRP)]
        return copy_to(src, dst, x_pair, ((g,), (g,)), (x, y, pair, core))

    def x_y_copy(g, way, to):
        rows = pl.ds(g * GRP, GRP)
        at = ((way, g), (y_hi, g))
        return copy_to(stage.at[rows], x_land.at[rows, y_hi], x_y, at, (x, to, z, core))

    def x_keep_copy(g):
        rows = pl.ds(g * GRP, GRP)
        return pltpu.make_async_copy(stage.at[rows], x_land.at[rows, y_hi], x_y.at[1, y_hi, g])

    def x_y_arrived(g):
        rows = pl.ds(g * GRP, GRP)
        for b in range(2):
            at = ((0, g), (b, g))
            copy_to(
                stage.at[rows], x_land.at[rows, b], x_y, at, (x, across, z, core)
            ).wait_recv()

    def x_forward(g):
        @pl.when(core == 0)
        def _():
            x_y_copy(g, 0, across).start()
            x_keep_copy(g).start()

        @pl.when(core == 1)
        def _():
            x_y_copy(g, 0, up).start()
            x_y_copy(g, 1, down).start()

    def c_y_copy(way, to):
        at = ((way,), (y_hi,))
        return copy_to(send_c.at[to // 2], c_mid.at[:, y_hi], c_y, at, (x, to, z, core))

    def c_keep_copy():
        return pltpu.make_async_copy(send_c.at[y_hi], c_mid.at[:, y_hi], c_y.at[1, y_hi])

    def c_relay_copy(k):
        xd, zd = relay_of(x, z, k)
        src = c_mid.at[xd * 2 + zd // 4]
        return copy_to(src, c_land.at[k], c_relay, ((k,), (k,)), (xd, y, zd, core))

    def c_own_copy():
        return pltpu.make_async_copy(c_mid.at[x * 2 + z // 4], c_land.at[0], c_relay.at[1, 0])

    def c_pair_copy(g):
        src = c_land.at[pl.ds(g * GRP, GRP)]
        dst = c_land.at[pl.ds(HALF + g * GRP, GRP)]
        return copy_to(src, dst, c_pair, ((g,), (g,)), (x, y, pair, core))

    blocks = w_down.shape[0]
    w_part = blocks // 2

    def w_keep_copy():
        columns = pl.ds(pl.multiple_of(y_hi * half, 128), half)
        return pltpu.make_async_copy(w_down.at[:, :, columns], w_land.at[0], w_sem.at[1, 0])

    def w_beside_copy():
        columns = pl.ds(pl.multiple_of(beside // 2 * half, 128), half)
        rows = pl.ds(core * w_part, w_part)
        src, dst = w_down.at[rows, :, columns], w_land.at[1, rows]
        return copy_to(src, dst, w_sem, ((1,), (1,)), (x, beside, z, core))

    def w_core_copy():
        rows = pl.ds(core * w_part, w_part)
        ref = w_land.at[1, rows]
        return copy_to(ref, ref, w_sem, ((2,), (2,)), (x, y, z, 1 - core))

    def h_copy(j):
        rows = pl.ds(j * chunk, chunk)
        at = ((j,), (j,))
        return copy_to(hidden.at[0, rows], hidden.at[1, rows], h_sem, at, (x, across, z, core))

    def b_copy(j):
        rows = pl.ds(j * chunk, chunk)
        at = ((j,), (j,))
        return copy_to(back.at[0, rows], back.at[1, rows], b_sem, at, (x, across, z, core))

    def p_copy(k):
        xd, zd = source_of(x, z, k)
        dst = parts_in.at[x * NZ + z]
        return copy_to(parts.at[k], dst, p_sem, ((k,), (k,)), (xd, y, zd, core))

    def p_own_copy():
        return pltpu.make_async_copy(parts.at[0], parts_in.at[x * NZ + z], p_sem.at[1, 0])

    def s_copy(way, to):
        at = ((way,), (y_hi,))
        return copy_to(sums.at[to // 2], out_rows.at[y_hi], s_sem, at, (x, to, z, core))

    def s_keep_copy():
        return pltpu.make_async_copy(sums.at[y_hi], out_rows.at[y_hi], s_sem.at[1, y_hi])

    def core_copy(i):
        at = ((i,), (i,))
        return copy_to(mine.at[i], theirs.at[i], core_sem, at, (x, y, z, 1 - core))

    outs = (out_gate, out_up)
    tile_blocks = TILE // rows_each

    def t_copy(i, w, part, to_y, to_core):
        rows = pl.ds((part * tiles + i) * tile_blocks, tile_blocks)
        at = ((w, to_core, i), (w, part, i))
        return copy_to(
            total.at[i, w], outs[w].at[rows], t_sem, at, (x, to_y, z, to_core)
        )

    def t_keep_copy(i, w):
        rows = pl.ds(i * tile_blocks, tile_blocks)
        return pltpu.make_async_copy(total.at[i, w], outs[w].at[rows], t_sem.at[1, w, 0, i])

    def flat(block):
        return block.reshape(-1, block.shape[-1])

    x_own_copy().start()
    w_keep_copy().start()
    loop(1, HALF, lambda k: x_relay_copy(k).start())

    @pl.when(core == 0)
    def _():
        c_y_copy(0, across).start()
        c_keep_copy().start()

    @pl.when(core == 1)
    def _():
        c_y_copy(0, up).start()
        c_y_copy(1, down).start()

    w_beside_copy().start()

    x_own_copy().wait()

    def x_near(g):
        loop(jnp.maximum(g * GRP, 1), g * GRP + GRP, lambda k: x_relay_copy(k).wait_recv())
        x_pair_copy(g).start()
        x_forward(g)

    loop(0, NG // 2, x_near)

    for b in range(2):
        at = ((0,), (b,))
        copy_to(
            send_c.at[0], c_mid.at[:, b], c_y, at, (x, across, z, core)
        ).wait_recv()
    c_own_copy().start()
    loop(1, HALF, lambda k: c_relay_copy(k).start())

    def x_far(g):
        x_pair_copy(g).wait_recv()
        x_forward(g + NG // 2)

    loop(0, NG // 2, x_far)

    w_beside_copy().wait_recv()
    w_core_copy().start()
    c_own_copy().wait()

    def c_near(g):
        loop(jnp.maximum(g * GRP, 1), g * GRP + GRP, lambda k: c_relay_copy(k).wait_recv())
        c_pair_copy(g).start()

    loop(0, NG // 2, c_near)

    def forward_pass(j):
        loop(j * NG // CHUNKS, (j + 1) * NG // CHUNKS, x_y_arrived)
        rows = pl.ds(j * chunk, chunk)
        block = flat(x_land[pl.ds(j * chunk_slots, chunk_slots)])
        x_rows[rows] = block
        a = jnp.dot(block, w_gate[...], preferred_element_type=f32)
        b = jnp.dot(block, w_up[...], preferred_element_type=f32)
        pre[0, rows] = a
        pre[1, rows] = b
        hidden[0, rows] = (a * jax.nn.sigmoid(a) * b).astype(bf16)
        h_copy(j).start()

    loop(0, CHUNKS, forward_pass)

    w_keep_copy().wait()
    w_core_copy().wait_recv()
    for i in range(2):
        w_rows[pl.ds(i * hid, hid)] = flat(w_land[i])

    def output_pass(j):
        h_copy(j).wait_recv()
        rows = pl.ds(j * chunk, chunk)
        both = jnp.dot(hidden[0, rows], w_rows[:hid], preferred_element_type=f32)
        both += jnp.dot(hidden[1, rows], w_rows[hid:], preferred_element_type=f32)
        both = both.reshape(chunk_slots, 2, rows_each, half).astype(bf16)
        parts[pl.ds(j * chunk_slots, chunk_slots)] = both
        first = j * chunk_slots
        loop(jnp.maximum(first, 1), first + chunk_slots, lambda k: p_copy(k).start())

    def back_pass(j):
        @pl.when(j >= CHUNKS // 2)
        def _():
            per = NG // CHUNKS
            first = j * per - NG // 2
            loop(first, first + per, lambda g: c_pair_copy(g).wait_recv())

        rows = pl.ds(j * chunk, chunk)
        block = flat(c_land[pl.ds(j * chunk_slots, chunk_slots)])
        contract = (((1,), (1,)), ((), ()))
        own = lax.dot_general(block, w_rows[:hid], contract, preferred_element_type=f32)
        other = lax.dot_general(block, w_rows[hid:], contract, preferred_element_type=f32)
        back[0, rows] = other.astype(bf16)
        b_copy(j).start()
        grad[rows] = own

    def pass_j(j):
        output_pass(j)
        back_pass(j)

    loop(0, CHUNKS, pass_j)
    p_own_copy().start()

    def grad_pass(j):
        b_copy(j).wait_recv()
        rows = pl.ds(j * chunk, chunk)
        whole = grad[rows] + back[1, rows].astype(f32)
        a, b = pre[0, rows], pre[1, rows]
        s = jax.nn.sigmoid(a)
        slopes[rows, :hid] = (whole * b * s * (1.0 + a * (1.0 - s))).astype(bf16)
        slopes[rows, hid:] = (whole * a * s).astype(bf16)

    loop(0, CHUNKS, grad_pass)

    def term(tile):
        columns = pl.ds(pl.multiple_of(tile * TILE, TILE), TILE)
        contract = (((0,), (0,)), ((), ()))
        return lax.dot_general(
            x_rows[:, columns], slopes[...], contract, preferred_element_type=f32
        )

    def term_for_other(i):
        mine[i] = term((1 - core) * tiles + i).astype(bf16)
        core_copy(i).start()

    loop(0, tiles, term_for_other)

    def term_here(i):
        own = term(core * tiles + i)
        core_copy(i).wait_recv()
        both = (own + theirs[i].astype(f32)).reshape(tile_blocks, rows_each, 2 * hid)
        total[i, 0] = both[:, :, :hid].astype(bf16)
        total[i, 1] = both[:, :, hid:].astype(bf16)

        @pl.when(core == 0)
        def _():
            for w in range(2):
                t_copy(i, w, 0, partner, 1).start()
                t_keep_copy(i, w).start()

        @pl.when(core == 1)
        def _():
            for w in range(2):
                t_copy(i, w, 1, partner, 1).start()
                t_copy(i, w, 1, y, 0).start()

    loop(0, tiles, term_here)

    p_own_copy().wait()
    loop(1, PLANE, lambda k: p_copy(k).wait_recv())
    experts = sums.shape[1]
    copies = PLANE // experts

    def sum_expert(e):
        acc = parts_in[e * copies].astype(f32)
        for i in range(1, copies):
            acc += parts_in[e * copies + i].astype(f32)
        for b in range(2):
            sums[b, e] = acc[b].astype(bf16)

    loop(0, experts, sum_expert)

    @pl.when(core == 0)
    def _():
        s_copy(0, across).start()
        s_keep_copy().start()

    @pl.when(core == 1)
    def _():
        s_copy(0, up).start()
        s_copy(1, down).start()

    loop(1, HALF, lambda k: x_relay_copy(k).wait_send())
    loop(1, HALF, lambda k: c_relay_copy(k).wait_send())
    loop(0, NG // 2, lambda g: x_pair_copy(g).wait_send())
    loop(0, NG // 2, lambda g: c_pair_copy(g).wait_send())
    loop(0, CHUNKS, lambda j: h_copy(j).wait_send())
    loop(0, CHUNKS, lambda j: b_copy(j).wait_send())
    loop(1, PLANE, lambda k: p_copy(k).wait_send())
    loop(0, tiles, lambda i: core_copy(i).wait_send())
    w_beside_copy().wait_send()
    w_core_copy().wait_send()
    for b in range(2):
        at = ((0,), (b,))
        copy_to(sums.at[0], out_rows.at[b], s_sem, at, (x, across, z, core)).wait_recv()

    @pl.when(core == 0)
    def _():
        loop(0, NG, lambda g: x_y_copy(g, 0, across).wait_send())
        c_y_copy(0, across).wait_send()
        s_copy(0, across).wait_send()

        def finish(i):
            for w in range(2):
                t_copy(i, w, 0, partner, 1).wait_send()
                t_keep_copy(i, w).wait()
                t_copy(i, w, 1, y, 0).wait_recv()

        loop(0, tiles, finish)

    @pl.when(core == 1)
    def _():
        def finish_rows(g):
            x_y_copy(g, 0, up).wait_send()
            x_y_copy(g, 1, down).wait_send()

        loop(0, NG, finish_rows)
        c_y_copy(0, up).wait_send()
        c_y_copy(1, down).wait_send()
        s_copy(0, up).wait_send()
        s_copy(1, down).wait_send()

        def finish(i):
            for w in range(2):
                t_copy(i, w, 1, partner, 1).wait()
                t_copy(i, w, 1, y, 0).wait_send()
                t_copy(i, w, 0, partner, 1).wait_recv()

        loop(0, tiles, finish)


def run_ranks(send_x, send_c, w_gate, w_up, w_down):
    experts, rows, width = send_x.shape
    hid = w_gate.shape[1]
    half, hid_blocks, all_rows = width // 2, hid // rows, 2 * PLANE * rows
    tiles = half // TILE
    bf16, f32, vmem, dma = jnp.bfloat16, jnp.float32, pltpu.VMEM, pltpu.SemaphoreType.DMA
    grad = jax.ShapeDtypeStruct((width // rows, rows, hid), bf16)
    return pl.pallas_call(
        rank_kernel,
        out_shape=(jax.ShapeDtypeStruct((2, experts, rows, half), bf16), grad, grad),
        in_specs=[pl.BlockSpec(memory_space=vmem)] * 5,
        out_specs=[pl.BlockSpec(memory_space=pl.ANY)] * 3,
        scratch_shapes=[
            vmem((PLANE, rows, width), bf16),
            vmem((PLANE, 2, rows, width), bf16),
            vmem((all_rows, width), bf16),
            vmem((experts, 2, rows, half), bf16),
            vmem((PLANE, 2, rows, half), bf16),
            vmem((2, hid_blocks, rows, half), bf16),
            vmem((2 * hid, half), bf16),
            vmem((2, all_rows, hid), f32),
            vmem((2, all_rows, hid), bf16),
            vmem((2, all_rows, hid), bf16),
            vmem((all_rows, hid), f32),
            vmem((all_rows, 2 * hid), bf16),
            vmem((PLANE, 2, rows, half), bf16),
            vmem((PLANE, 2, rows, half), bf16),
            vmem((2, experts, rows, half), bf16),
            vmem((tiles, TILE, 2 * hid), bf16),
            vmem((tiles, TILE, 2 * hid), bf16),
            vmem((tiles, 2, TILE // rows, rows, hid), bf16),
            dma((2, HALF)),
            dma((2, NG // 2)),
            dma((2, 2, NG)),
            dma((2, 2)),
            dma((2, HALF)),
            dma((2, NG // 2)),
            dma((2, 3)),
            dma((2, CHUNKS)),
            dma((2, CHUNKS)),
            dma((2, PLANE)),
            dma((2, 2)),
            dma((2, tiles)),
            dma((2, 2, 2, tiles)),
        ],
        compiler_params=pltpu.CompilerParams(
            collective_id=0, has_side_effects=True, vmem_limit_bytes=54 << 20
        ),
    )(send_x, send_c, w_gate, w_up, w_down)


def slot_tables(expert_ids, gate_values, flight_count, capacity):
    experts = jnp.arange(flight_count, dtype=jnp.int32)
    match = (expert_ids[:, :, None] == experts[None, None, :]).astype(jnp.float32)
    counted = jnp.sum(match, axis=1)
    before = jnp.cumsum(counted, axis=0) - counted
    places = jnp.arange(capacity, dtype=jnp.float32)
    slot_hit = counted[:, :, None] * (before[:, :, None] == places[None, None, :]).astype(
        jnp.float32
    )
    gate_each = jnp.sum(match * gate_values.astype(jnp.float32)[:, :, None], axis=1)
    return (match, slot_hit, gate_each)


def per_device(tokens, expert_ids, gate_values, cotangent, w_gate, w_up, w_down):
    device_count = lax.axis_size("expert")
    hidden_dev = w_gate.shape[1]
    slice_count = FFW // hidden_dev
    flight_count = device_count // slice_count
    width = tokens.shape[1]
    half = width // 2
    capacity = CAP
    f32, bf16 = jnp.float32, jnp.bfloat16
    row_contract = (((0,), (0,)), ((), ()))
    match, slot_hit, gate_each = slot_tables(expert_ids, gate_values, flight_count, capacity)
    hit_flat = slot_hit.reshape(slot_hit.shape[0], flight_count * capacity).astype(bf16)
    token_buf = lax.dot_general(hit_flat, tokens, row_contract, preferred_element_type=f32)
    cot_buf = lax.dot_general(hit_flat, cotangent, row_contract, preferred_element_type=f32)
    gate_buf = jnp.sum(slot_hit * gate_each[:, :, None], axis=0).reshape(-1, 1)
    send_x = token_buf.astype(bf16).reshape(flight_count, capacity, width)
    scaled = (gate_buf * cot_buf).astype(bf16)
    send_c = jnp.stack([scaled[:, :half], scaled[:, half:]])
    send_c = send_c.reshape(2, flight_count, capacity, half)
    w_blocks = w_down.reshape(-1, capacity, width)
    returned, grad_gate, grad_up = run_ranks(send_x, send_c, w_gate, w_up, w_blocks)

    returned = returned.reshape(2, -1, half)
    returned = jnp.concatenate([returned[0], returned[1]], axis=1)
    weight_hit = (slot_hit * gate_each[:, :, None]).astype(bf16).reshape(hit_flat.shape)
    mixed = jnp.dot(weight_hit, returned, preferred_element_type=f32).astype(bf16)
    values = jnp.sum(returned.astype(f32) * cot_buf, axis=1).reshape(flight_count, capacity)
    value_each = jnp.einsum("tec,ec->te", slot_hit, values, precision=lax.Precision.HIGHEST)
    gate_grad = jnp.einsum("tke,te->tk", match, value_each, precision=lax.Precision.HIGHEST)
    grad_shape = (1, width, hidden_dev)
    return (mixed, gate_grad, grad_gate.reshape(grad_shape), grad_up.reshape(grad_shape))


def solution(mesh):
    placed = (
        P(("pipe", "expert"), None),
        P(("pipe", "expert"), None),
        P(("pipe", "expert"), None),
        P(("pipe", "expert"), None),
        P(None, "expert"),
        P(None, "expert"),
        P("expert", None),
    )
    return jax.shard_map(
        per_device,
        mesh=mesh,
        in_specs=placed,
        out_specs=(
            P(("pipe", "expert"), None),
            P(("pipe", "expert"), None),
            P("pipe", None, "expert"),
            P("pipe", None, "expert"),
        ),
        check_vma=False,
    )
```

```python
import jax
import jax.numpy as jnp
from jax import lax
from jax.experimental import pallas as pl
from jax.experimental.pallas import tpu as pltpu
from jax.sharding import PartitionSpec as P

FFW = 2048
CAP = 8
MESH = pl.DeviceIdType.MESH
NX, NZ, NY = 4, 8, 4
PLANE = NX * NZ
PAIRS = NZ // 2
HALF = NX * PAIRS
GRP = 4
NG = PLANE // GRP
CHUNKS = 2
TILE = 256


def where_am_i():
    p, i = lax.axis_index("pipe"), lax.axis_index("expert")
    x, z, y_hi = i // (2 * NZ), (i // 2) % NZ, i % 2
    return p, x, 2 * y_hi + p // 2, z, p % 2


def device_at(x, y, z, core):
    return ((y % 2) * 2 + core, (x * NZ + z) * 2 + y // 2)


def source_of(x, z, k):
    sign = 1 - 2 * (z % 2)
    far, t, dx = k // HALF, k // NX % PAIRS, k % NX
    dz = far * (t + 1) - (1 - far) * t
    return (x + NX - dx) % NX, (z + NZ + sign * dz) % NZ


def relay_of(x, z, k):
    sign = 1 - 2 * (z % 2)
    t, dx = k // NX, k % NX
    dz = t * (1 - 2 * (t % 2))
    return (x + dx) % NX, (z + NZ + sign * dz) % NZ


def rank_kernel(
    send_x,
    send_c,
    w_gate,
    w_up,
    w_down,
    out_rows,
    out_gate,
    out_up,
    stage,
    x_land,
    x_rows,
    c_mid,
    c_land,
    w_land,
    w_rows,
    pre,
    hidden,
    back,
    grad,
    slopes,
    parts,
    parts_in,
    sums,
    mine,
    theirs,
    total,
    x_relay,
    x_pair,
    x_y,
    c_y,
    c_relay,
    c_pair,
    w_sem,
    h_sem,
    b_sem,
    p_sem,
    s_sem,
    core_sem,
    t_sem,
):
    p, x, y, z, core = where_am_i()
    up, down, across = (y + 1) % NY, (y + NY - 1) % NY, (y + 2) % NY
    partner, beside = y + 1 - 2 * (y % 2), (y + NY - 1 + 2 * (y % 2)) % NY
    pair = z + 1 - 2 * (z % 2)
    y_hi = y // 2
    f32, bf16 = jnp.float32, jnp.bfloat16
    slots, _, rows_each, width = x_land.shape
    half = width // 2
    hid = w_gate.shape[1]
    chunk_slots = slots // CHUNKS
    chunk = chunk_slots * 2 * rows_each
    tiles = theirs.shape[0]

    def copy_to(src, dst, sems, at, to):
        return pltpu.make_async_remote_copy(
            src_ref=src,
            dst_ref=dst,
            send_sem=sems.at[(0,) + at[0]],
            recv_sem=sems.at[(1,) + at[1]],
            device_id=device_at(*to),
            device_id_type=MESH,
        )

    def loop(first, last, body):
        def step(i, carry):
            body(i)
            return carry

        lax.fori_loop(first, last, step, 0)

    barrier = pltpu.get_barrier_semaphore()

    def greet(xd, yd, zd, to_core):
        pl.semaphore_signal(
            barrier, inc=1, device_id=device_at(xd, yd, zd, to_core), device_id_type=MESH
        )

    def greet_source(k):
        xs, zs = source_of(x, z, k)
        greet(xs, y, zs, core)

    loop(1, PLANE, greet_source)
    greet(x, across, z, core)
    greet(x, y, z, 1 - core)

    @pl.when(core == 0)
    def _():
        greet(x, beside, z, 0)

    @pl.when(core == 1)
    def _():
        greet(x, up, z, 1)
        greet(x, down, z, 1)
        greet(x, partner, z, 0)

    pl.semaphore_wait(barrier, PLANE + 3)

    def x_relay_copy(k):
        xd, zd = relay_of(x, z, k)
        src = send_x.at[xd * 2 + zd // 4]
        return copy_to(src, stage.at[k], x_relay, ((k,), (k,)), (xd, y, zd, core))

    def x_own_copy():
        return pltpu.make_async_copy(send_x.at[x * 2 + z // 4], stage.at[0], x_relay.at[1, 0])

    def x_pair_copy(g):
        src = stage.at[pl.ds(g * GRP, GRP)]
        dst = stage.at[pl.ds(HALF + g * GRP, GRP)]
        return copy_to(src, dst, x_pair, ((g,), (g,)), (x, y, pair, core))

    def x_y_copy(g, way, to):
        rows = pl.ds(g * GRP, GRP)
        at = ((way, g), (y_hi, g))
        return copy_to(stage.at[rows], x_land.at[rows, y_hi], x_y, at, (x, to, z, core))

    def x_keep_copy(g):
        rows = pl.ds(g * GRP, GRP)
        return pltpu.make_async_copy(stage.at[rows], x_land.at[rows, y_hi], x_y.at[1, y_hi, g])

    def x_y_arrived(g):
        rows = pl.ds(g * GRP, GRP)
        for b in range(2):
            at = ((0, g), (b, g))
            copy_to(
                stage.at[rows], x_land.at[rows, b], x_y, at, (x, across, z, core)
            ).wait_recv()

    def x_forward(g):
        @pl.when(core == 0)
        def _():
            x_y_copy(g, 0, across).start()
            x_keep_copy(g).start()

        @pl.when(core == 1)
        def _():
            x_y_copy(g, 0, up).start()
            x_y_copy(g, 1, down).start()

    def c_y_copy(way, to):
        at = ((way,), (y_hi,))
        return copy_to(send_c.at[to // 2], c_mid.at[:, y_hi], c_y, at, (x, to, z, core))

    def c_keep_copy():
        return pltpu.make_async_copy(send_c.at[y_hi], c_mid.at[:, y_hi], c_y.at[1, y_hi])

    def c_relay_copy(k):
        xd, zd = relay_of(x, z, k)
        src = c_mid.at[xd * 2 + zd // 4]
        return copy_to(src, c_land.at[k], c_relay, ((k,), (k,)), (xd, y, zd, core))

    def c_own_copy():
        return pltpu.make_async_copy(c_mid.at[x * 2 + z // 4], c_land.at[0], c_relay.at[1, 0])

    def c_pair_copy(g):
        src = c_land.at[pl.ds(g * GRP, GRP)]
        dst = c_land.at[pl.ds(HALF + g * GRP, GRP)]
        return copy_to(src, dst, c_pair, ((g,), (g,)), (x, y, pair, core))

    blocks = w_down.shape[0]
    w_part = blocks // 2

    def w_keep_copy():
        columns = pl.ds(pl.multiple_of(y_hi * half, 128), half)
        return pltpu.make_async_copy(w_down.at[:, :, columns], w_land.at[0], w_sem.at[1, 0])

    def w_beside_copy():
        columns = pl.ds(pl.multiple_of(beside // 2 * half, 128), half)
        rows = pl.ds(core * w_part, w_part)
        src, dst = w_down.at[rows, :, columns], w_land.at[1, rows]
        return copy_to(src, dst, w_sem, ((1,), (1,)), (x, beside, z, core))

    def w_core_copy():
        rows = pl.ds(core * w_part, w_part)
        ref = w_land.at[1, rows]
        return copy_to(ref, ref, w_sem, ((2,), (2,)), (x, y, z, 1 - core))

    def h_copy(j):
        rows = pl.ds(j * chunk, chunk)
        at = ((j,), (j,))
        return copy_to(hidden.at[0, rows], hidden.at[1, rows], h_sem, at, (x, across, z, core))

    def b_copy(j):
        rows = pl.ds(j * chunk, chunk)
        at = ((j,), (j,))
        return copy_to(back.at[0, rows], back.at[1, rows], b_sem, at, (x, across, z, core))

    def p_copy(k):
        xd, zd = source_of(x, z, k)
        dst = parts_in.at[x * NZ + z]
        return copy_to(parts.at[k], dst, p_sem, ((k,), (x * NZ + z,)), (xd, y, zd, core))

    def p_own_copy():
        return pltpu.make_async_copy(
            parts.at[0], parts_in.at[x * NZ + z], p_sem.at[1, x * NZ + z]
        )

    def s_copy(e, way, to):
        at = ((way, e), (y_hi, e))
        return copy_to(sums.at[to // 2, e], out_rows.at[y_hi, e], s_sem, at, (x, to, z, core))

    def s_keep_copy(e):
        return pltpu.make_async_copy(sums.at[y_hi, e], out_rows.at[y_hi, e], s_sem.at[1, y_hi, e])

    def core_copy(i):
        at = ((i,), (i,))
        return copy_to(mine.at[i], theirs.at[i], core_sem, at, (x, y, z, 1 - core))

    outs = (out_gate, out_up)
    tile_blocks = TILE // rows_each

    def t_copy(i, w, part, to_y, to_core):
        rows = pl.ds((part * tiles + i) * tile_blocks, tile_blocks)
        at = ((w, to_core, i), (w, part, i))
        return copy_to(
            total.at[i, w], outs[w].at[rows], t_sem, at, (x, to_y, z, to_core)
        )

    def t_keep_copy(i, w):
        rows = pl.ds(i * tile_blocks, tile_blocks)
        return pltpu.make_async_copy(total.at[i, w], outs[w].at[rows], t_sem.at[1, w, 0, i])

    def flat(block):
        return block.reshape(-1, block.shape[-1])

    @pl.when(core == 0)
    def _():
        c_y_copy(0, across).start()
        c_keep_copy().start()

    @pl.when(core == 1)
    def _():
        c_y_copy(0, up).start()
        c_y_copy(1, down).start()

    x_own_copy().start()
    loop(1, HALF, lambda k: x_relay_copy(k).start())
    w_keep_copy().start()
    w_beside_copy().start()

    def x_near(g):
        loop(jnp.maximum(g * GRP, 1), g * GRP + GRP, lambda k: x_relay_copy(k).wait_recv())
        x_pair_copy(g).start()
        x_forward(g)

    def x_far(g):
        x_pair_copy(g).wait_recv()
        x_forward(g + NG // 2)

    x_own_copy().wait()
    x_near(0)

    def x_next(g):
        x_near(g)
        x_far(g - 1)

    loop(1, NG // 2, x_next)
    for b in range(2):
        at = ((0,), (b,))
        copy_to(
            send_c.at[0], c_mid.at[:, b], c_y, at, (x, across, z, core)
        ).wait_recv()
    c_own_copy().start()
    loop(1, HALF, lambda k: c_relay_copy(k).start())
    x_far(NG // 2 - 1)
    w_beside_copy().wait_recv()
    w_core_copy().start()
    c_own_copy().wait()

    def c_near(g):
        loop(jnp.maximum(g * GRP, 1), g * GRP + GRP, lambda k: c_relay_copy(k).wait_recv())
        c_pair_copy(g).start()

    loop(0, NG // 2, c_near)

    def forward_pass(j):
        loop(j * NG // CHUNKS, (j + 1) * NG // CHUNKS, x_y_arrived)
        rows = pl.ds(j * chunk, chunk)
        block = flat(x_land[pl.ds(j * chunk_slots, chunk_slots)])
        x_rows[rows] = block
        a = jnp.dot(block, w_gate[...], preferred_element_type=f32)
        b = jnp.dot(block, w_up[...], preferred_element_type=f32)
        pre[0, rows] = a
        pre[1, rows] = b
        hidden[0, rows] = (a * jax.nn.sigmoid(a) * b).astype(bf16)
        h_copy(j).start()

    def output_pass(j):
        h_copy(j).wait_recv()
        rows = pl.ds(j * chunk, chunk)
        both = jnp.dot(hidden[0, rows], w_rows[:hid], preferred_element_type=f32)
        both += jnp.dot(hidden[1, rows], w_rows[hid:], preferred_element_type=f32)
        both = both.reshape(chunk_slots, 2, rows_each, half).astype(bf16)
        parts[pl.ds(j * chunk_slots, chunk_slots)] = both

    def send_parts(j):
        first = j * chunk_slots
        loop(jnp.maximum(first, 1), first + chunk_slots, lambda k: p_copy(k).start())

    def back_pass(j):
        @pl.when(j >= CHUNKS // 2)
        def _():
            per = NG // CHUNKS
            first = j * per - NG // 2
            loop(first, first + per, lambda g: c_pair_copy(g).wait_recv())

        rows = pl.ds(j * chunk, chunk)
        block = flat(c_land[pl.ds(j * chunk_slots, chunk_slots)])
        contract = (((1,), (1,)), ((), ()))
        own = lax.dot_general(block, w_rows[:hid], contract, preferred_element_type=f32)
        other = lax.dot_general(block, w_rows[hid:], contract, preferred_element_type=f32)
        back[0, rows] = other.astype(bf16)
        b_copy(j).start()
        grad[rows] = own

    def grad_pass(j):
        b_copy(j).wait_recv()
        rows = pl.ds(j * chunk, chunk)
        whole = grad[rows] + back[1, rows].astype(f32)
        a, b = pre[0, rows], pre[1, rows]
        s = jax.nn.sigmoid(a)
        slopes[rows, :hid] = (whole * b * s * (1.0 + a * (1.0 - s))).astype(bf16)
        slopes[rows, hid:] = (whole * a * s).astype(bf16)

    def prepare_weights():
        w_keep_copy().wait()
        w_core_copy().wait_recv()
        for i in range(2):
            w_rows[pl.ds(i * hid, hid)] = flat(w_land[i])

    loop(0, 1, forward_pass)
    prepare_weights()
    loop(0, 1, back_pass)
    loop(1, 2, forward_pass)
    loop(0, 1, output_pass)
    loop(0, 1, grad_pass)
    loop(1, 2, back_pass)
    p_own_copy().start()
    loop(0, 1, send_parts)
    loop(1, 2, output_pass)
    loop(1, 2, send_parts)
    loop(1, 2, grad_pass)


    def term(tile):
        columns = pl.ds(pl.multiple_of(tile * TILE, TILE), TILE)
        contract = (((0,), (0,)), ((), ()))
        return lax.dot_general(
            x_rows[:, columns], slopes[...], contract, preferred_element_type=f32
        )

    def term_here(i):
        mine[i] = term((1 - core) * tiles + i).astype(bf16)
        core_copy(i).start()
        own = term(core * tiles + i)
        core_copy(i).wait_recv()
        both = (own + theirs[i].astype(f32)).reshape(tile_blocks, rows_each, 2 * hid)
        total[i, 0] = both[:, :, :hid].astype(bf16)
        total[i, 1] = both[:, :, hid:].astype(bf16)

        @pl.when(core == 0)
        def _():
            for w in range(2):
                t_copy(i, w, 0, partner, 1).start()
                t_keep_copy(i, w).start()

        @pl.when(core == 1)
        def _():
            for w in range(2):
                t_copy(i, w, 1, partner, 1).start()
                t_copy(i, w, 1, y, 0).start()

    loop(0, tiles, term_here)

    experts = sums.shape[1]
    copies = PLANE // experts

    def sum_expert(e):
        def arrived(i):
            copy_to(
                parts.at[0], parts_in.at[i], p_sem, ((0,), (i,)), (x, across, z, core)
            ).wait_recv()

        loop(e * copies, e * copies + copies, arrived)
        acc = parts_in[e * copies].astype(f32)
        for i in range(1, copies):
            acc += parts_in[e * copies + i].astype(f32)
        for b in range(2):
            sums[b, e] = acc[b].astype(bf16)

        @pl.when(core == 0)
        def _():
            s_copy(e, 0, across).start()
            s_keep_copy(e).start()

        @pl.when(core == 1)
        def _():
            s_copy(e, 0, up).start()
            s_copy(e, 1, down).start()

    loop(0, experts, sum_expert)

    loop(1, HALF, lambda k: x_relay_copy(k).wait_send())
    loop(1, HALF, lambda k: c_relay_copy(k).wait_send())
    loop(0, NG // 2, lambda g: x_pair_copy(g).wait_send())
    loop(0, NG // 2, lambda g: c_pair_copy(g).wait_send())
    loop(0, CHUNKS, lambda j: h_copy(j).wait_send())
    loop(0, CHUNKS, lambda j: b_copy(j).wait_send())
    loop(1, PLANE, lambda k: p_copy(k).wait_send())
    loop(0, tiles, lambda i: core_copy(i).wait_send())
    w_beside_copy().wait_send()
    w_core_copy().wait_send()

    def s_arrived(e):
        for b in range(2):
            at = ((0, e), (b, e))
            copy_to(
                sums.at[0, e], out_rows.at[b, e], s_sem, at, (x, across, z, core)
            ).wait_recv()

    loop(0, experts, s_arrived)

    @pl.when(core == 0)
    def _():
        loop(0, NG, lambda g: x_y_copy(g, 0, across).wait_send())
        c_y_copy(0, across).wait_send()
        loop(0, experts, lambda e: s_copy(e, 0, across).wait_send())

        def finish(i):
            for w in range(2):
                t_copy(i, w, 0, partner, 1).wait_send()
                t_keep_copy(i, w).wait()
                t_copy(i, w, 1, y, 0).wait_recv()

        loop(0, tiles, finish)

    @pl.when(core == 1)
    def _():
        def finish_rows(g):
            x_y_copy(g, 0, up).wait_send()
            x_y_copy(g, 1, down).wait_send()

        loop(0, NG, finish_rows)
        c_y_copy(0, up).wait_send()
        c_y_copy(1, down).wait_send()
        loop(0, experts, lambda e: s_copy(e, 0, up).wait_send())
        loop(0, experts, lambda e: s_copy(e, 1, down).wait_send())

        def finish(i):
            for w in range(2):
                t_copy(i, w, 1, partner, 1).wait()
                t_copy(i, w, 1, y, 0).wait_send()
                t_copy(i, w, 0, partner, 1).wait_recv()

        loop(0, tiles, finish)


def run_ranks(send_x, send_c, w_gate, w_up, w_down):
    experts, rows, width = send_x.shape
    hid = w_gate.shape[1]
    half, hid_blocks, all_rows = width // 2, hid // rows, 2 * PLANE * rows
    tiles = half // TILE
    bf16, f32, vmem, dma = jnp.bfloat16, jnp.float32, pltpu.VMEM, pltpu.SemaphoreType.DMA
    grad = jax.ShapeDtypeStruct((width // rows, rows, hid), bf16)
    return pl.pallas_call(
        rank_kernel,
        out_shape=(jax.ShapeDtypeStruct((2, experts, rows, half), bf16), grad, grad),
        in_specs=[pl.BlockSpec(memory_space=vmem)] * 5,
        out_specs=[pl.BlockSpec(memory_space=pl.ANY)] * 3,
        scratch_shapes=[
            vmem((PLANE, rows, width), bf16),
            vmem((PLANE, 2, rows, width), bf16),
            vmem((all_rows, width), bf16),
            vmem((experts, 2, rows, half), bf16),
            vmem((PLANE, 2, rows, half), bf16),
            vmem((2, hid_blocks, rows, half), bf16),
            vmem((2 * hid, half), bf16),
            vmem((2, all_rows, hid), f32),
            vmem((2, all_rows, hid), bf16),
            vmem((2, all_rows, hid), bf16),
            vmem((all_rows, hid), f32),
            vmem((all_rows, 2 * hid), bf16),
            vmem((PLANE, 2, rows, half), bf16),
            vmem((PLANE, 2, rows, half), bf16),
            vmem((2, experts, rows, half), bf16),
            vmem((tiles, TILE, 2 * hid), bf16),
            vmem((tiles, TILE, 2 * hid), bf16),
            vmem((tiles, 2, TILE // rows, rows, hid), bf16),
            dma((2, HALF)),
            dma((2, NG // 2)),
            dma((2, 2, NG)),
            dma((2, 2)),
            dma((2, HALF)),
            dma((2, NG // 2)),
            dma((2, 3)),
            dma((2, CHUNKS)),
            dma((2, CHUNKS)),
            dma((2, PLANE)),
            dma((2, 2, experts)),
            dma((2, tiles)),
            dma((2, 2, 2, tiles)),
        ],
        compiler_params=pltpu.CompilerParams(
            collective_id=0, has_side_effects=True, vmem_limit_bytes=54 << 20
        ),
    )(send_x, send_c, w_gate, w_up, w_down)


def slot_tables(expert_ids, gate_values, flight_count, capacity):
    experts = jnp.arange(flight_count, dtype=jnp.int32)
    match = (expert_ids[:, :, None] == experts[None, None, :]).astype(jnp.float32)
    counted = jnp.sum(match, axis=1)
    before = jnp.cumsum(counted, axis=0) - counted
    places = jnp.arange(capacity, dtype=jnp.float32)
    slot_hit = counted[:, :, None] * (before[:, :, None] == places[None, None, :]).astype(
        jnp.float32
    )
    gate_each = jnp.sum(match * gate_values.astype(jnp.float32)[:, :, None], axis=1)
    return (match, slot_hit, gate_each)


def per_device(tokens, expert_ids, gate_values, cotangent, w_gate, w_up, w_down):
    device_count = lax.axis_size("expert")
    hidden_dev = w_gate.shape[1]
    slice_count = FFW // hidden_dev
    flight_count = device_count // slice_count
    width = tokens.shape[1]
    half = width // 2
    capacity = CAP
    f32, bf16 = jnp.float32, jnp.bfloat16
    row_contract = (((0,), (0,)), ((), ()))
    match, slot_hit, gate_each = slot_tables(expert_ids, gate_values, flight_count, capacity)
    hit_flat = slot_hit.reshape(slot_hit.shape[0], flight_count * capacity).astype(bf16)
    token_buf = lax.dot_general(hit_flat, tokens, row_contract, preferred_element_type=f32)
    cot_buf = lax.dot_general(hit_flat, cotangent, row_contract, preferred_element_type=f32)
    gate_buf = jnp.sum(slot_hit * gate_each[:, :, None], axis=0).reshape(-1, 1)
    send_x = token_buf.astype(bf16).reshape(flight_count, capacity, width)
    scaled = (gate_buf * cot_buf).astype(bf16)
    send_c = jnp.stack([scaled[:, :half], scaled[:, half:]])
    send_c = send_c.reshape(2, flight_count, capacity, half)
    w_blocks = w_down.reshape(-1, capacity, width)
    returned, grad_gate, grad_up = run_ranks(send_x, send_c, w_gate, w_up, w_blocks)

    returned = returned.reshape(2, -1, half)
    returned = jnp.concatenate([returned[0], returned[1]], axis=1)
    weight_hit = (slot_hit * gate_each[:, :, None]).astype(bf16).reshape(hit_flat.shape)
    mixed = jnp.dot(weight_hit, returned, preferred_element_type=f32).astype(bf16)
    values = jnp.sum(returned.astype(f32) * cot_buf, axis=1).reshape(flight_count, capacity)
    value_each = jnp.einsum("tec,ec->te", slot_hit, values, precision=lax.Precision.HIGHEST)
    gate_grad = jnp.einsum("tke,te->tk", match, value_each, precision=lax.Precision.HIGHEST)
    grad_shape = (1, width, hidden_dev)
    return (mixed, gate_grad, grad_gate.reshape(grad_shape), grad_up.reshape(grad_shape))


def solution(mesh):
    placed = (
        P(("pipe", "expert"), None),
        P(("pipe", "expert"), None),
        P(("pipe", "expert"), None),
        P(("pipe", "expert"), None),
        P(None, "expert"),
        P(None, "expert"),
        P("expert", None),
    )
    return jax.shard_map(
        per_device,
        mesh=mesh,
        in_specs=placed,
        out_specs=(
            P(("pipe", "expert"), None),
            P(("pipe", "expert"), None),
            P("pipe", None, "expert"),
            P("pipe", None, "expert"),
        ),
        check_vma=False,
    )
```

```python
import jax
import jax.numpy as jnp
from jax import lax
from jax.experimental import pallas as pl
from jax.experimental.pallas import tpu as pltpu
from jax.sharding import PartitionSpec as P

FFW = 2048
CAP = 8
MESH = pl.DeviceIdType.MESH
NX, NZ, NY = 4, 8, 4
PLANE = NX * NZ
PAIRS = NZ // 2
HALF = NX * PAIRS
GRP = 4
NG = PLANE // GRP
CHUNKS = 2
TILE = 256


def where_am_i():
    p, i = lax.axis_index("pipe"), lax.axis_index("expert")
    x, z, y_hi = i // (2 * NZ), (i // 2) % NZ, i % 2
    return p, x, 2 * y_hi + p // 2, z, p % 2


def device_at(x, y, z, core):
    return ((y % 2) * 2 + core, (x * NZ + z) * 2 + y // 2)


def source_of(x, z, k):
    sign = 1 - 2 * (z % 2)
    far, t, dx = k // HALF, k // NX % PAIRS, k % NX
    dz = far * (t + 1) - (1 - far) * t
    return (x + NX - dx) % NX, (z + NZ + sign * dz) % NZ


def relay_of(x, z, k):
    sign = 1 - 2 * (z % 2)
    t, dx = k // NX, k % NX
    dz = t * (1 - 2 * (t % 2))
    return (x + dx) % NX, (z + NZ + sign * dz) % NZ


def rank_kernel(
    hits,
    gates,
    tokens,
    cotangent,
    w_gate,
    w_up,
    w_down,
    out_rows,
    out_gate,
    out_up,
    out_cots,
    send_x,
    send_c,
    w_in,
    w_cols,
    stage,
    x_land,
    x_rows,
    c_mid,
    c_land,
    w_land,
    w_rows,
    pre,
    hidden,
    back,
    grad,
    slopes,
    parts,
    parts_in,
    sums,
    mine,
    theirs,
    total,
    x_relay,
    x_pair,
    x_y,
    c_y,
    c_relay,
    c_pair,
    w_sem,
    in_sem,
    h_sem,
    b_sem,
    p_sem,
    s_sem,
    core_sem,
    t_sem,
):
    p, x, y, z, core = where_am_i()
    up, down, across = (y + 1) % NY, (y + NY - 1) % NY, (y + 2) % NY
    partner, beside = y + 1 - 2 * (y % 2), (y + NY - 1 + 2 * (y % 2)) % NY
    pair = z + 1 - 2 * (z % 2)
    y_hi = y // 2
    f32, bf16 = jnp.float32, jnp.bfloat16
    slots, _, rows_each, width = x_land.shape
    half = width // 2
    hid = w_gate.shape[-1]
    chunk_slots = slots // CHUNKS
    chunk = chunk_slots * 2 * rows_each
    tiles = theirs.shape[0]

    def copy_to(src, dst, sems, at, to):
        return pltpu.make_async_remote_copy(
            src_ref=src,
            dst_ref=dst,
            send_sem=sems.at[(0,) + at[0]],
            recv_sem=sems.at[(1,) + at[1]],
            device_id=device_at(*to),
            device_id_type=MESH,
        )

    def loop(first, last, body):
        def step(i, carry):
            body(i)
            return carry

        lax.fori_loop(first, last, step, 0)

    def w_load(i):
        return pltpu.make_async_copy((w_gate, w_up)[i], w_in.at[i], in_sem.at[i])

    for i in range(2):
        w_load(i).start()
    barrier = pltpu.get_barrier_semaphore()

    def greet(xd, yd, zd, to_core):
        pl.semaphore_signal(
            barrier, inc=1, device_id=device_at(xd, yd, zd, to_core), device_id_type=MESH
        )

    def greet_source(k):
        xs, zs = source_of(x, z, k)
        greet(xs, y, zs, core)

    loop(1, PLANE, greet_source)
    greet(x, across, z, core)
    greet(x, y, z, 1 - core)

    @pl.when(core == 0)
    def _():
        greet(x, beside, z, 0)

    @pl.when(core == 1)
    def _():
        greet(x, up, z, 1)
        greet(x, down, z, 1)
        greet(x, partner, z, 0)

    for c in range(width // TILE):
        columns = slice(c * TILE, (c + 1) * TILE)
        contract = (((0,), (0,)), ((), ()))
        picked = lax.dot_general(
            hits[...], tokens[:, columns], contract, preferred_element_type=f32
        )
        send_x[:, :, columns] = picked.reshape(-1, rows_each, TILE).astype(bf16)
        picked = lax.dot_general(
            hits[...], cotangent[:, columns], contract, preferred_element_type=f32
        )
        out_cots[:, columns] = picked.astype(bf16)
        scaled = (gates[...] * picked).reshape(-1, rows_each, TILE).astype(bf16)
        send_c[c // tiles, :, :, c % tiles * TILE : (c % tiles + 1) * TILE] = scaled

    pl.semaphore_wait(barrier, PLANE + 3)

    def x_relay_copy(k):
        xd, zd = relay_of(x, z, k)
        src = send_x.at[xd * 2 + zd // 4]
        return copy_to(src, stage.at[k], x_relay, ((k,), (k,)), (xd, y, zd, core))

    def x_own_copy():
        return pltpu.make_async_copy(send_x.at[x * 2 + z // 4], stage.at[0], x_relay.at[1, 0])

    def x_pair_copy(g):
        src = stage.at[pl.ds(g * GRP, GRP)]
        dst = stage.at[pl.ds(HALF + g * GRP, GRP)]
        return copy_to(src, dst, x_pair, ((g,), (g,)), (x, y, pair, core))

    def x_y_copy(g, way, to):
        rows = pl.ds(g * GRP, GRP)
        at = ((way, g), (y_hi, g))
        return copy_to(stage.at[rows], x_land.at[rows, y_hi], x_y, at, (x, to, z, core))

    def x_keep_copy(g):
        rows = pl.ds(g * GRP, GRP)
        return pltpu.make_async_copy(stage.at[rows], x_land.at[rows, y_hi], x_y.at[1, y_hi, g])

    def x_y_arrived(g):
        rows = pl.ds(g * GRP, GRP)
        for b in range(2):
            at = ((0, g), (b, g))
            copy_to(
                stage.at[rows], x_land.at[rows, b], x_y, at, (x, across, z, core)
            ).wait_recv()

    def x_forward(g):
        @pl.when(core == 0)
        def _():
            x_y_copy(g, 0, across).start()
            x_keep_copy(g).start()

        @pl.when(core == 1)
        def _():
            x_y_copy(g, 0, up).start()
            x_y_copy(g, 1, down).start()

    def c_y_copy(way, to):
        at = ((way,), (y_hi,))
        return copy_to(send_c.at[to // 2], c_mid.at[:, y_hi], c_y, at, (x, to, z, core))

    def c_keep_copy():
        return pltpu.make_async_copy(send_c.at[y_hi], c_mid.at[:, y_hi], c_y.at[1, y_hi])

    def c_relay_copy(k):
        xd, zd = relay_of(x, z, k)
        src = c_mid.at[xd * 2 + zd // 4]
        return copy_to(src, c_land.at[k], c_relay, ((k,), (k,)), (xd, y, zd, core))

    def c_own_copy():
        return pltpu.make_async_copy(c_mid.at[x * 2 + z // 4], c_land.at[0], c_relay.at[1, 0])

    def c_pair_copy(g):
        src = c_land.at[pl.ds(g * GRP, GRP)]
        dst = c_land.at[pl.ds(HALF + g * GRP, GRP)]
        return copy_to(src, dst, c_pair, ((g,), (g,)), (x, y, pair, core))

    blocks = w_down.shape[0]
    w_part = blocks // 2

    def w_keep_copy():
        columns = pl.ds(pl.multiple_of(y_hi * half, 128), half)
        return pltpu.make_async_copy(w_down.at[:, :, columns], w_land.at[0], w_sem.at[1, 0])

    def w_beside_copy():
        columns = pl.ds(pl.multiple_of(beside // 2 * half, 128), half)
        rows = pl.ds(core * w_part, w_part)
        src, dst = w_down.at[rows, :, columns], w_land.at[1, rows]
        return copy_to(src, dst, w_sem, ((1,), (1,)), (x, beside, z, core))

    def w_core_copy():
        rows = pl.ds(core * w_part, w_part)
        ref = w_land.at[1, rows]
        return copy_to(ref, ref, w_sem, ((2,), (2,)), (x, y, z, 1 - core))

    def h_copy(j):
        rows = pl.ds(j * chunk, chunk)
        at = ((j,), (j,))
        return copy_to(hidden.at[0, rows], hidden.at[1, rows], h_sem, at, (x, across, z, core))

    def b_copy(j):
        rows = pl.ds(j * chunk, chunk)
        at = ((j,), (j,))
        return copy_to(back.at[0, rows], back.at[1, rows], b_sem, at, (x, across, z, core))

    def p_copy(k):
        xd, zd = source_of(x, z, k)
        dst = parts_in.at[x * NZ + z]
        return copy_to(parts.at[k], dst, p_sem, ((k,), (x * NZ + z,)), (xd, y, zd, core))

    def p_own_copy():
        return pltpu.make_async_copy(
            parts.at[0], parts_in.at[x * NZ + z], p_sem.at[1, x * NZ + z]
        )

    own_columns = pl.ds(pl.multiple_of(y_hi * half, 128), half)

    def s_copy(e, way, to):
        at = ((way, e), (y_hi, e))
        dst = out_rows.at[e, :, own_columns]
        return copy_to(sums.at[to // 2, e], dst, s_sem, at, (x, to, z, core))

    def s_keep_copy(e):
        dst = out_rows.at[e, :, own_columns]
        return pltpu.make_async_copy(sums.at[y_hi, e], dst, s_sem.at[1, y_hi, e])

    def core_copy(i):
        at = ((i,), (i,))
        return copy_to(mine.at[i], theirs.at[i], core_sem, at, (x, y, z, 1 - core))

    outs = (out_gate, out_up)
    tile_blocks = TILE // rows_each

    def t_copy(i, w, part, to_y, to_core):
        rows = pl.ds((part * tiles + i) * tile_blocks, tile_blocks)
        at = ((w, to_core, i), (w, part, i))
        return copy_to(
            total.at[i, w], outs[w].at[rows], t_sem, at, (x, to_y, z, to_core)
        )

    def t_keep_copy(i, w):
        rows = pl.ds(i * tile_blocks, tile_blocks)
        return pltpu.make_async_copy(total.at[i, w], outs[w].at[rows], t_sem.at[1, w, 0, i])

    def flat(block):
        return block.reshape(-1, block.shape[-1])

    @pl.when(core == 0)
    def _():
        c_y_copy(0, across).start()
        c_keep_copy().start()

    @pl.when(core == 1)
    def _():
        c_y_copy(0, up).start()
        c_y_copy(1, down).start()

    x_own_copy().start()
    loop(1, HALF, lambda k: x_relay_copy(k).start())
    w_keep_copy().start()
    w_beside_copy().start()

    def x_near(g):
        loop(jnp.maximum(g * GRP, 1), g * GRP + GRP, lambda k: x_relay_copy(k).wait_recv())
        x_pair_copy(g).start()
        x_forward(g)

    def x_far(g):
        x_pair_copy(g).wait_recv()
        x_forward(g + NG // 2)

    x_own_copy().wait()
    x_near(0)

    def x_next(g):
        x_near(g)
        x_far(g - 1)

    loop(1, NG // 2, x_next)
    for b in range(2):
        at = ((0,), (b,))
        copy_to(
            send_c.at[0], c_mid.at[:, b], c_y, at, (x, across, z, core)
        ).wait_recv()
    c_own_copy().start()
    loop(1, HALF, lambda k: c_relay_copy(k).start())
    x_far(NG // 2 - 1)
    w_beside_copy().wait_recv()
    w_core_copy().start()
    c_own_copy().wait()

    def c_near(g):
        loop(jnp.maximum(g * GRP, 1), g * GRP + GRP, lambda k: c_relay_copy(k).wait_recv())
        c_pair_copy(g).start()

    loop(0, NG // 2, c_near)

    def forward_pass(j):
        loop(j * NG // CHUNKS, (j + 1) * NG // CHUNKS, x_y_arrived)
        rows = pl.ds(j * chunk, chunk)
        block = flat(x_land[pl.ds(j * chunk_slots, chunk_slots)])
        x_rows[rows] = block
        a = jnp.dot(block, w_cols[0], preferred_element_type=f32)
        b = jnp.dot(block, w_cols[1], preferred_element_type=f32)
        pre[0, rows] = a
        pre[1, rows] = b
        hidden[0, rows] = (a * jax.nn.sigmoid(a) * b).astype(bf16)
        h_copy(j).start()

    def output_pass(j):
        h_copy(j).wait_recv()
        rows = pl.ds(j * chunk, chunk)
        both = jnp.dot(hidden[0, rows], w_rows[:hid], preferred_element_type=f32)
        both += jnp.dot(hidden[1, rows], w_rows[hid:], preferred_element_type=f32)
        both = both.reshape(chunk_slots, 2, rows_each, half).astype(bf16)
        parts[pl.ds(j * chunk_slots, chunk_slots)] = both

    def send_parts(j):
        first = j * chunk_slots
        loop(jnp.maximum(first, 1), first + chunk_slots, lambda k: p_copy(k).start())

    def back_pass(j):
        @pl.when(j >= CHUNKS // 2)
        def _():
            per = NG // CHUNKS
            first = j * per - NG // 2
            loop(first, first + per, lambda g: c_pair_copy(g).wait_recv())

        rows = pl.ds(j * chunk, chunk)
        block = flat(c_land[pl.ds(j * chunk_slots, chunk_slots)])
        contract = (((1,), (1,)), ((), ()))
        own = lax.dot_general(block, w_rows[:hid], contract, preferred_element_type=f32)
        other = lax.dot_general(block, w_rows[hid:], contract, preferred_element_type=f32)
        back[0, rows] = other.astype(bf16)
        b_copy(j).start()
        grad[rows] = own

    def grad_pass(j):
        b_copy(j).wait_recv()
        rows = pl.ds(j * chunk, chunk)
        whole = grad[rows] + back[1, rows].astype(f32)
        a, b = pre[0, rows], pre[1, rows]
        s = jax.nn.sigmoid(a)
        slopes[rows, :hid] = (whole * b * s * (1.0 + a * (1.0 - s))).astype(bf16)
        slopes[rows, hid:] = (whole * a * s).astype(bf16)

    def prepare_weights():
        w_keep_copy().wait()
        w_core_copy().wait_recv()
        for i in range(2):
            w_rows[pl.ds(i * hid, hid)] = flat(w_land[i])

    for i in range(2):
        w_load(i).wait()

        def lay_out(r, i=i):
            w_cols[i, pl.ds(r * TILE, TILE)] = flat(w_in[i, pl.ds(r * tile_blocks, tile_blocks)])

        loop(0, width // TILE, lay_out)

    loop(0, 1, forward_pass)
    prepare_weights()
    loop(0, 1, back_pass)
    loop(1, 2, forward_pass)
    loop(0, 1, output_pass)
    loop(0, 1, grad_pass)
    loop(1, 2, back_pass)
    p_own_copy().start()
    loop(0, 1, send_parts)
    loop(1, 2, output_pass)
    loop(1, 2, send_parts)
    loop(1, 2, grad_pass)


    def term(tile):
        columns = pl.ds(pl.multiple_of(tile * TILE, TILE), TILE)
        contract = (((0,), (0,)), ((), ()))
        return lax.dot_general(
            x_rows[:, columns], slopes[...], contract, preferred_element_type=f32
        )

    def term_here(i):
        mine[i] = term((1 - core) * tiles + i).astype(bf16)
        core_copy(i).start()
        own = term(core * tiles + i)
        core_copy(i).wait_recv()
        both = (own + theirs[i].astype(f32)).reshape(tile_blocks, rows_each, 2 * hid)
        total[i, 0] = both[:, :, :hid].astype(bf16)
        total[i, 1] = both[:, :, hid:].astype(bf16)

        @pl.when(core == 0)
        def _():
            for w in range(2):
                t_copy(i, w, 0, partner, 1).start()
                t_keep_copy(i, w).start()

        @pl.when(core == 1)
        def _():
            for w in range(2):
                t_copy(i, w, 1, partner, 1).start()
                t_copy(i, w, 1, y, 0).start()

    loop(0, tiles, term_here)

    experts = sums.shape[1]
    copies = PLANE // experts

    def sum_expert(e):
        def arrived(i):
            copy_to(
                parts.at[0], parts_in.at[i], p_sem, ((0,), (i,)), (x, across, z, core)
            ).wait_recv()

        loop(e * copies, e * copies + copies, arrived)
        acc = parts_in[e * copies].astype(f32)
        for i in range(1, copies):
            acc += parts_in[e * copies + i].astype(f32)
        for b in range(2):
            sums[b, e] = acc[b].astype(bf16)

        @pl.when(core == 0)
        def _():
            s_copy(e, 0, across).start()
            s_keep_copy(e).start()

        @pl.when(core == 1)
        def _():
            s_copy(e, 0, up).start()
            s_copy(e, 1, down).start()

    loop(0, experts, sum_expert)

    loop(1, HALF, lambda k: x_relay_copy(k).wait_send())
    loop(1, HALF, lambda k: c_relay_copy(k).wait_send())
    loop(0, NG // 2, lambda g: x_pair_copy(g).wait_send())
    loop(0, NG // 2, lambda g: c_pair_copy(g).wait_send())
    loop(0, CHUNKS, lambda j: h_copy(j).wait_send())
    loop(0, CHUNKS, lambda j: b_copy(j).wait_send())
    loop(1, PLANE, lambda k: p_copy(k).wait_send())
    loop(0, tiles, lambda i: core_copy(i).wait_send())
    w_beside_copy().wait_send()
    w_core_copy().wait_send()

    def s_arrived(e):
        for b in range(2):
            at = ((0, e), (b, e))
            dst = out_rows.at[e, :, pl.ds(b * half, half)]
            copy_to(sums.at[0, e], dst, s_sem, at, (x, across, z, core)).wait_recv()

    loop(0, experts, s_arrived)

    @pl.when(core == 0)
    def _():
        loop(0, NG, lambda g: x_y_copy(g, 0, across).wait_send())
        c_y_copy(0, across).wait_send()
        loop(0, experts, lambda e: s_copy(e, 0, across).wait_send())

        def finish(i):
            for w in range(2):
                t_copy(i, w, 0, partner, 1).wait_send()
                t_keep_copy(i, w).wait()
                t_copy(i, w, 1, y, 0).wait_recv()

        loop(0, tiles, finish)

    @pl.when(core == 1)
    def _():
        def finish_rows(g):
            x_y_copy(g, 0, up).wait_send()
            x_y_copy(g, 1, down).wait_send()

        loop(0, NG, finish_rows)
        c_y_copy(0, up).wait_send()
        c_y_copy(1, down).wait_send()
        loop(0, experts, lambda e: s_copy(e, 0, up).wait_send())
        loop(0, experts, lambda e: s_copy(e, 1, down).wait_send())

        def finish(i):
            for w in range(2):
                t_copy(i, w, 1, partner, 1).wait()
                t_copy(i, w, 1, y, 0).wait_send()
                t_copy(i, w, 0, partner, 1).wait_recv()

        loop(0, tiles, finish)


def run_ranks(hits, gates, tokens, cotangent, w_gate, w_up, w_down):
    all_slots, width = hits.shape[1], tokens.shape[1]
    rows, hid = w_gate.shape[1:]
    experts = all_slots // rows
    half, hid_blocks, all_rows = width // 2, hid // rows, 2 * PLANE * rows
    tiles = half // TILE
    bf16, f32, vmem, dma = jnp.bfloat16, jnp.float32, pltpu.VMEM, pltpu.SemaphoreType.DMA
    grad = jax.ShapeDtypeStruct((width // rows, rows, hid), bf16)
    in_vmem, anywhere = pl.BlockSpec(memory_space=vmem), pl.BlockSpec(memory_space=pl.ANY)
    return pl.pallas_call(
        rank_kernel,
        out_shape=(
            jax.ShapeDtypeStruct((experts, rows, width), bf16),
            grad,
            grad,
            jax.ShapeDtypeStruct((all_slots, width), bf16),
        ),
        in_specs=[in_vmem] * 4 + [anywhere] * 3,
        out_specs=[anywhere] * 3 + [in_vmem],
        scratch_shapes=[
            vmem((experts, rows, width), bf16),
            vmem((2, experts, rows, half), bf16),
            vmem((2, width // rows, rows, hid), bf16),
            vmem((2, width, hid), bf16),
            vmem((PLANE, rows, width), bf16),
            vmem((PLANE, 2, rows, width), bf16),
            vmem((all_rows, width), bf16),
            vmem((experts, 2, rows, half), bf16),
            vmem((PLANE, 2, rows, half), bf16),
            vmem((2, hid_blocks, rows, half), bf16),
            vmem((2 * hid, half), bf16),
            vmem((2, all_rows, hid), f32),
            vmem((2, all_rows, hid), bf16),
            vmem((2, all_rows, hid), bf16),
            vmem((all_rows, hid), f32),
            vmem((all_rows, 2 * hid), bf16),
            vmem((PLANE, 2, rows, half), bf16),
            vmem((PLANE, 2, rows, half), bf16),
            vmem((2, experts, rows, half), bf16),
            vmem((tiles, TILE, 2 * hid), bf16),
            vmem((tiles, TILE, 2 * hid), bf16),
            vmem((tiles, 2, TILE // rows, rows, hid), bf16),
            dma((2, HALF)),
            dma((2, NG // 2)),
            dma((2, 2, NG)),
            dma((2, 2)),
            dma((2, HALF)),
            dma((2, NG // 2)),
            dma((2, 3)),
            dma((2,)),
            dma((2, CHUNKS)),
            dma((2, CHUNKS)),
            dma((2, PLANE)),
            dma((2, 2, experts)),
            dma((2, tiles)),
            dma((2, 2, 2, tiles)),
        ],
        compiler_params=pltpu.CompilerParams(
            collective_id=0, has_side_effects=True, vmem_limit_bytes=54 << 20
        ),
    )(hits, gates, tokens, cotangent, w_gate, w_up, w_down)


def slot_tables(expert_ids, gate_values, flight_count, capacity):
    experts = jnp.arange(flight_count, dtype=jnp.int32)
    match = (expert_ids[:, :, None] == experts[None, None, :]).astype(jnp.float32)
    counted = jnp.sum(match, axis=1)
    before = jnp.cumsum(counted, axis=0) - counted
    places = jnp.arange(capacity, dtype=jnp.float32)
    slot_hit = counted[:, :, None] * (before[:, :, None] == places[None, None, :]).astype(
        jnp.float32
    )
    gate_each = jnp.sum(match * gate_values.astype(jnp.float32)[:, :, None], axis=1)
    return (match, slot_hit, gate_each)


def per_device(tokens, expert_ids, gate_values, cotangent, w_gate, w_up, w_down):
    device_count = lax.axis_size("expert")
    hidden_dev = w_gate.shape[1]
    slice_count = FFW // hidden_dev
    flight_count = device_count // slice_count
    width = tokens.shape[1]
    capacity = CAP
    f32, bf16 = jnp.float32, jnp.bfloat16
    match, slot_hit, gate_each = slot_tables(expert_ids, gate_values, flight_count, capacity)
    hit_flat = slot_hit.reshape(slot_hit.shape[0], flight_count * capacity).astype(bf16)
    gate_buf = jnp.sum(slot_hit * gate_each[:, :, None], axis=0).reshape(-1, 1)

    def to_blocks(weight):
        return weight.reshape(-1, capacity, weight.shape[1])

    returned, grad_gate, grad_up, cot_buf = run_ranks(
        hit_flat,
        gate_buf,
        tokens,
        cotangent,
        to_blocks(w_gate),
        to_blocks(w_up),
        to_blocks(w_down),
    )
    returned = returned.reshape(-1, width)
    weight_hit = (slot_hit * gate_each[:, :, None]).astype(bf16).reshape(hit_flat.shape)
    mixed = jnp.dot(weight_hit, returned, preferred_element_type=f32).astype(bf16)
    values = jnp.sum(returned.astype(f32) * cot_buf.astype(f32), axis=1).reshape(flight_count, capacity)
    value_each = jnp.einsum("tec,ec->te", slot_hit, values, precision=lax.Precision.HIGHEST)
    gate_grad = jnp.einsum("tke,te->tk", match, value_each, precision=lax.Precision.HIGHEST)
    grad_shape = (1, width, hidden_dev)
    return (mixed, gate_grad, grad_gate.reshape(grad_shape), grad_up.reshape(grad_shape))


def solution(mesh):
    placed = (
        P(("pipe", "expert"), None),
        P(("pipe", "expert"), None),
        P(("pipe", "expert"), None),
        P(("pipe", "expert"), None),
        P(None, "expert"),
        P(None, "expert"),
        P("expert", None),
    )
    return jax.shard_map(
        per_device,
        mesh=mesh,
        in_specs=placed,
        out_specs=(
            P(("pipe", "expert"), None),
            P(("pipe", "expert"), None),
            P("pipe", None, "expert"),
            P("pipe", None, "expert"),
        ),
        check_vma=False,
    )
```

```python
import jax
import jax.numpy as jnp
from jax import lax
from jax.experimental import pallas as pl
from jax.experimental.pallas import tpu as pltpu
from jax.sharding import PartitionSpec as P

FFW = 2048
CAP = 8
MESH = pl.DeviceIdType.MESH
NX, NZ, NY = 4, 8, 4
PLANE = NX * NZ
PAIRS = NZ // 2
HALF = NX * PAIRS
GRP = 4
NG = PLANE // GRP
CHUNKS = 2
TILE = 256


def where_am_i():
    p, i = lax.axis_index("pipe"), lax.axis_index("expert")
    x, z, y_hi = i // (2 * NZ), (i // 2) % NZ, i % 2
    return p, x, 2 * y_hi + p // 2, z, p % 2


def device_at(x, y, z, core):
    return ((y % 2) * 2 + core, (x * NZ + z) * 2 + y // 2)


def source_of(x, z, k):
    sign = 1 - 2 * (z % 2)
    far, t, dx = k // HALF, k // NX % PAIRS, k % NX
    dz = far * (t + 1) - (1 - far) * t
    return (x + NX - dx) % NX, (z + NZ + sign * dz) % NZ


def relay_of(x, z, k):
    sign = 1 - 2 * (z % 2)
    t, dx = k // NX, k % NX
    dz = t * (1 - 2 * (t % 2))
    return (x + dx) % NX, (z + NZ + sign * dz) % NZ


def rank_kernel(
    hits,
    gates,
    tokens,
    cotangent,
    w_gate,
    w_up,
    w_down,
    out_rows,
    out_gate,
    out_up,
    out_cots,
    send_x,
    send_c,
    w_in,
    w_cols,
    stage,
    x_land,
    x_rows,
    c_mid,
    c_land,
    w_land,
    w_rows,
    pre,
    hidden,
    back,
    grad,
    slopes,
    parts,
    parts_in,
    sums,
    mine,
    theirs,
    total,
    x_relay,
    x_pair,
    x_y,
    c_y,
    c_relay,
    c_pair,
    w_sem,
    in_sem,
    h_sem,
    b_sem,
    p_sem,
    s_sem,
    core_sem,
    t_sem,
):
    p, x, y, z, core = where_am_i()
    up, down, across = (y + 1) % NY, (y + NY - 1) % NY, (y + 2) % NY
    partner, beside = y + 1 - 2 * (y % 2), (y + NY - 1 + 2 * (y % 2)) % NY
    pair = z + 1 - 2 * (z % 2)
    y_hi = y // 2
    f32, bf16 = jnp.float32, jnp.bfloat16
    slots, _, rows_each, width = x_land.shape
    half = width // 2
    hid = w_gate.shape[-1]
    chunk_slots = slots // CHUNKS
    chunk = chunk_slots * 2 * rows_each
    tiles = theirs.shape[0]

    def copy_to(src, dst, sems, at, to):
        return pltpu.make_async_remote_copy(
            src_ref=src,
            dst_ref=dst,
            send_sem=sems.at[(0,) + at[0]],
            recv_sem=sems.at[(1,) + at[1]],
            device_id=device_at(*to),
            device_id_type=MESH,
        )

    def loop(first, last, body):
        def step(i, carry):
            body(i)
            return carry

        lax.fori_loop(first, last, step, 0)

    def w_load(i):
        return pltpu.make_async_copy((w_gate, w_up)[i], w_in.at[i], in_sem.at[i])

    for i in range(2):
        w_load(i).start()
    barrier = pltpu.get_barrier_semaphore()

    def greet(xd, yd, zd, to_core):
        pl.semaphore_signal(
            barrier, inc=1, device_id=device_at(xd, yd, zd, to_core), device_id_type=MESH
        )

    def greet_source(k):
        xs, zs = source_of(x, z, k)
        greet(xs, y, zs, core)

    loop(1, PLANE, greet_source)
    greet(x, across, z, core)
    greet(x, y, z, 1 - core)

    @pl.when(core == 0)
    def _():
        greet(x, beside, z, 0)

    @pl.when(core == 1)
    def _():
        greet(x, up, z, 1)
        greet(x, down, z, 1)
        greet(x, partner, z, 0)

    for c in range(width // TILE):
        columns = slice(c * TILE, (c + 1) * TILE)
        contract = (((0,), (0,)), ((), ()))
        picked = lax.dot_general(
            hits[...], tokens[:, columns], contract, preferred_element_type=f32
        )
        send_x[:, :, columns] = picked.reshape(-1, rows_each, TILE).astype(bf16)
        picked = lax.dot_general(
            hits[...], cotangent[:, columns], contract, preferred_element_type=f32
        )
        out_cots[:, columns] = picked.astype(bf16)
        scaled = (gates[...] * picked).reshape(-1, rows_each, TILE).astype(bf16)
        send_c[c // tiles, :, :, c % tiles * TILE : (c % tiles + 1) * TILE] = scaled

    pl.semaphore_wait(barrier, PLANE + 3)

    def x_relay_copy(k):
        xd, zd = relay_of(x, z, k)
        src = send_x.at[xd * 2 + zd // 4]
        return copy_to(src, stage.at[k], x_relay, ((k,), (k,)), (xd, y, zd, core))

    def x_own_copy():
        return pltpu.make_async_copy(send_x.at[x * 2 + z // 4], stage.at[0], x_relay.at[1, 0])

    def x_pair_copy(g):
        src = stage.at[pl.ds(g * GRP, GRP)]
        dst = stage.at[pl.ds(HALF + g * GRP, GRP)]
        return copy_to(src, dst, x_pair, ((g,), (g,)), (x, y, pair, core))

    def x_y_copy(g, way, to):
        rows = pl.ds(g * GRP, GRP)
        at = ((way, g), (y_hi, g))
        return copy_to(stage.at[rows], x_land.at[rows, y_hi], x_y, at, (x, to, z, core))

    def x_keep_copy(g):
        rows = pl.ds(g * GRP, GRP)
        return pltpu.make_async_copy(stage.at[rows], x_land.at[rows, y_hi], x_y.at[1, y_hi, g])

    def x_y_arrived(g):
        rows = pl.ds(g * GRP, GRP)
        for b in range(2):
            at = ((0, g), (b, g))
            copy_to(
                stage.at[rows], x_land.at[rows, b], x_y, at, (x, across, z, core)
            ).wait_recv()

    def x_forward(g):
        @pl.when(core == 0)
        def _():
            x_y_copy(g, 0, across).start()
            x_keep_copy(g).start()

        @pl.when(core == 1)
        def _():
            x_y_copy(g, 0, up).start()
            x_y_copy(g, 1, down).start()

    def c_y_copy(way, to):
        at = ((way,), (y_hi,))
        return copy_to(send_c.at[to // 2], c_mid.at[:, y_hi], c_y, at, (x, to, z, core))

    def c_keep_copy():
        return pltpu.make_async_copy(send_c.at[y_hi], c_mid.at[:, y_hi], c_y.at[1, y_hi])

    def c_relay_copy(k):
        xd, zd = relay_of(x, z, k)
        src = c_mid.at[xd * 2 + zd // 4]
        return copy_to(src, c_land.at[k], c_relay, ((k,), (k,)), (xd, y, zd, core))

    def c_own_copy():
        return pltpu.make_async_copy(c_mid.at[x * 2 + z // 4], c_land.at[0], c_relay.at[1, 0])

    def c_pair_copy(g):
        src = c_land.at[pl.ds(g * GRP, GRP)]
        dst = c_land.at[pl.ds(HALF + g * GRP, GRP)]
        return copy_to(src, dst, c_pair, ((g,), (g,)), (x, y, pair, core))

    blocks = w_down.shape[0]
    w_part = blocks // 2

    def w_keep_copy():
        columns = pl.ds(pl.multiple_of(y_hi * half, 128), half)
        return pltpu.make_async_copy(w_down.at[:, :, columns], w_land.at[0], w_sem.at[1, 0])

    def w_beside_copy():
        columns = pl.ds(pl.multiple_of(beside // 2 * half, 128), half)
        rows = pl.ds(core * w_part, w_part)
        src, dst = w_down.at[rows, :, columns], w_land.at[1, rows]
        return copy_to(src, dst, w_sem, ((1,), (1,)), (x, beside, z, core))

    def w_core_copy():
        rows = pl.ds(core * w_part, w_part)
        ref = w_land.at[1, rows]
        return copy_to(ref, ref, w_sem, ((2,), (2,)), (x, y, z, 1 - core))

    def h_copy(j):
        rows = pl.ds(j * chunk, chunk)
        at = ((j,), (j,))
        return copy_to(hidden.at[0, rows], hidden.at[1, rows], h_sem, at, (x, across, z, core))

    def b_copy(j):
        rows = pl.ds(j * (chunk // 2), chunk // 2)
        at = ((j,), (j,))
        return copy_to(back.at[0, rows], back.at[1, rows], b_sem, at, (x, across, z, core))

    def p_copy(k):
        xd, zd = source_of(x, z, k)
        dst = parts_in.at[x * NZ + z]
        return copy_to(parts.at[k], dst, p_sem, ((k,), (x * NZ + z,)), (xd, y, zd, core))

    def p_own_copy():
        return pltpu.make_async_copy(
            parts.at[0], parts_in.at[x * NZ + z], p_sem.at[1, x * NZ + z]
        )

    own_columns = pl.ds(pl.multiple_of(y_hi * half, 128), half)

    def s_copy(e, way, to):
        at = ((way, e), (y_hi, e))
        dst = out_rows.at[e, :, own_columns]
        return copy_to(sums.at[to // 2, e], dst, s_sem, at, (x, to, z, core))

    def s_keep_copy(e):
        dst = out_rows.at[e, :, own_columns]
        return pltpu.make_async_copy(sums.at[y_hi, e], dst, s_sem.at[1, y_hi, e])

    def core_copy(i):
        at = ((i,), (i,))
        return copy_to(mine.at[i], theirs.at[i], core_sem, at, (x, y, z, 1 - core))

    outs = (out_gate, out_up)
    tile_blocks = TILE // rows_each

    def t_copy(i, w, part, to_y, to_core):
        rows = pl.ds((part * tiles + i) * tile_blocks, tile_blocks)
        at = ((w, to_core, i), (w, part, i))
        return copy_to(
            total.at[i, w], outs[w].at[rows], t_sem, at, (x, to_y, z, to_core)
        )

    def t_keep_copy(i, w):
        rows = pl.ds(i * tile_blocks, tile_blocks)
        return pltpu.make_async_copy(total.at[i, w], outs[w].at[rows], t_sem.at[1, w, 0, i])

    def flat(block):
        return block.reshape(-1, block.shape[-1])

    @pl.when(core == 0)
    def _():
        c_y_copy(0, across).start()
        c_keep_copy().start()

    @pl.when(core == 1)
    def _():
        c_y_copy(0, up).start()
        c_y_copy(1, down).start()

    x_own_copy().start()
    loop(1, HALF, lambda k: x_relay_copy(k).start())
    w_keep_copy().start()
    w_beside_copy().start()

    def x_near(g):
        loop(jnp.maximum(g * GRP, 1), g * GRP + GRP, lambda k: x_relay_copy(k).wait_recv())
        x_pair_copy(g).start()
        x_forward(g)

    def x_far(g):
        x_pair_copy(g).wait_recv()
        x_forward(g + NG // 2)

    x_own_copy().wait()
    x_near(0)

    def x_next(g):
        x_near(g)
        x_far(g - 1)

    loop(1, NG // 2, x_next)
    for b in range(2):
        at = ((0,), (b,))
        copy_to(
            send_c.at[0], c_mid.at[:, b], c_y, at, (x, across, z, core)
        ).wait_recv()
    c_own_copy().start()
    loop(1, HALF, lambda k: c_relay_copy(k).start())
    x_far(NG // 2 - 1)
    w_beside_copy().wait_recv()
    w_core_copy().start()
    c_own_copy().wait()

    def c_near(g):
        loop(jnp.maximum(g * GRP, 1), g * GRP + GRP, lambda k: c_relay_copy(k).wait_recv())
        c_pair_copy(g).start()

    loop(0, NG // 2, c_near)

    def forward_pass(j):
        loop(j * NG // CHUNKS, (j + 1) * NG // CHUNKS, x_y_arrived)
        rows = pl.ds(j * chunk, chunk)
        block = flat(x_land[pl.ds(j * chunk_slots, chunk_slots)])
        x_rows[rows] = block
        a = jnp.dot(block, w_cols[0], preferred_element_type=f32)
        b = jnp.dot(block, w_cols[1], preferred_element_type=f32)
        pre[0, rows] = a
        pre[1, rows] = b
        hidden[0, rows] = (a * jax.nn.sigmoid(a) * b).astype(bf16)
        h_copy(j).start()

    def output_pass(j):
        h_copy(j).wait_recv()
        rows = pl.ds(j * chunk, chunk)
        both = jnp.dot(hidden[0, rows], w_rows[:hid], preferred_element_type=f32)
        both += jnp.dot(hidden[1, rows], w_rows[hid:], preferred_element_type=f32)
        both = both.reshape(chunk_slots, 2, rows_each, half).astype(bf16)
        parts[pl.ds(j * chunk_slots, chunk_slots)] = both

    def send_parts(j):
        first = j * chunk_slots
        loop(jnp.maximum(first, 1), first + chunk_slots, lambda k: p_copy(k).start())

    def back_pass(j):
        @pl.when(j >= CHUNKS // 2)
        def _():
            per = NG // CHUNKS
            first = j * per - NG // 2
            loop(first, first + per, lambda g: c_pair_copy(g).wait_recv())

        rows = pl.ds(j * chunk, chunk)
        block = flat(c_land[pl.ds(j * chunk_slots, chunk_slots)])
        contract = (((1,), (1,)), ((), ()))
        other = lax.dot_general(block, w_rows[hid:], contract, preferred_element_type=f32)
        back[0, rows] = other.astype(bf16)
        b_copy(2 * j).start()
        b_copy(2 * j + 1).start()
        own = lax.dot_general(block, w_rows[:hid], contract, preferred_element_type=f32)
        grad[rows] = own

    def grad_pass(j):
        b_copy(j).wait_recv()
        rows = pl.ds(j * (chunk // 2), chunk // 2)
        whole = grad[rows] + back[1, rows].astype(f32)
        a, b = pre[0, rows], pre[1, rows]
        s = jax.nn.sigmoid(a)
        slopes[rows, :hid] = (whole * b * s * (1.0 + a * (1.0 - s))).astype(bf16)
        slopes[rows, hid:] = (whole * a * s).astype(bf16)

    def prepare_weights():
        w_keep_copy().wait()
        w_core_copy().wait_recv()
        for i in range(2):
            w_rows[pl.ds(i * hid, hid)] = flat(w_land[i])

    for i in range(2):
        w_load(i).wait()

        def lay_out(r, i=i):
            w_cols[i, pl.ds(r * TILE, TILE)] = flat(w_in[i, pl.ds(r * tile_blocks, tile_blocks)])

        loop(0, width // TILE, lay_out)

    loop(0, 1, forward_pass)
    prepare_weights()
    loop(0, 1, back_pass)
    loop(1, 2, forward_pass)
    loop(0, 1, output_pass)
    loop(0, 2, grad_pass)
    loop(1, 2, back_pass)
    p_own_copy().start()
    loop(0, 1, send_parts)
    loop(1, 2, output_pass)
    loop(1, 2, send_parts)
    loop(2, 4, grad_pass)


    def term(tile):
        columns = pl.ds(pl.multiple_of(tile * TILE, TILE), TILE)
        contract = (((0,), (0,)), ((), ()))
        return lax.dot_general(
            x_rows[:, columns], slopes[...], contract, preferred_element_type=f32
        )

    def term_here(i):
        mine[i] = term((1 - core) * tiles + i).astype(bf16)
        core_copy(i).start()
        own = term(core * tiles + i)
        core_copy(i).wait_recv()
        both = (own + theirs[i].astype(f32)).reshape(tile_blocks, rows_each, 2 * hid)
        total[i, 0] = both[:, :, :hid].astype(bf16)
        total[i, 1] = both[:, :, hid:].astype(bf16)

        @pl.when(core == 0)
        def _():
            for w in range(2):
                t_copy(i, w, 0, partner, 1).start()
                t_keep_copy(i, w).start()

        @pl.when(core == 1)
        def _():
            for w in range(2):
                t_copy(i, w, 1, partner, 1).start()
                t_copy(i, w, 1, y, 0).start()

    loop(0, tiles, term_here)

    experts = sums.shape[1]
    copies = PLANE // experts

    def sum_expert(e):
        def arrived(i):
            copy_to(
                parts.at[0], parts_in.at[i], p_sem, ((0,), (i,)), (x, across, z, core)
            ).wait_recv()

        loop(e * copies, e * copies + copies, arrived)
        acc = parts_in[e * copies].astype(f32)
        for i in range(1, copies):
            acc += parts_in[e * copies + i].astype(f32)
        for b in range(2):
            sums[b, e] = acc[b].astype(bf16)

        @pl.when(core == 0)
        def _():
            s_copy(e, 0, across).start()
            s_keep_copy(e).start()

        @pl.when(core == 1)
        def _():
            s_copy(e, 0, up).start()
            s_copy(e, 1, down).start()

    loop(0, experts, sum_expert)

    loop(1, HALF, lambda k: x_relay_copy(k).wait_send())
    loop(1, HALF, lambda k: c_relay_copy(k).wait_send())
    loop(0, NG // 2, lambda g: x_pair_copy(g).wait_send())
    loop(0, NG // 2, lambda g: c_pair_copy(g).wait_send())
    loop(0, CHUNKS, lambda j: h_copy(j).wait_send())
    loop(0, 2 * CHUNKS, lambda j: b_copy(j).wait_send())
    loop(1, PLANE, lambda k: p_copy(k).wait_send())
    loop(0, tiles, lambda i: core_copy(i).wait_send())
    w_beside_copy().wait_send()
    w_core_copy().wait_send()

    def s_arrived(e):
        for b in range(2):
            at = ((0, e), (b, e))
            dst = out_rows.at[e, :, pl.ds(b * half, half)]
            copy_to(sums.at[0, e], dst, s_sem, at, (x, across, z, core)).wait_recv()

    loop(0, experts, s_arrived)

    @pl.when(core == 0)
    def _():
        loop(0, NG, lambda g: x_y_copy(g, 0, across).wait_send())
        c_y_copy(0, across).wait_send()
        loop(0, experts, lambda e: s_copy(e, 0, across).wait_send())

        def finish(i):
            for w in range(2):
                t_copy(i, w, 0, partner, 1).wait_send()
                t_keep_copy(i, w).wait()
                t_copy(i, w, 1, y, 0).wait_recv()

        loop(0, tiles, finish)

    @pl.when(core == 1)
    def _():
        def finish_rows(g):
            x_y_copy(g, 0, up).wait_send()
            x_y_copy(g, 1, down).wait_send()

        loop(0, NG, finish_rows)
        c_y_copy(0, up).wait_send()
        c_y_copy(1, down).wait_send()
        loop(0, experts, lambda e: s_copy(e, 0, up).wait_send())
        loop(0, experts, lambda e: s_copy(e, 1, down).wait_send())

        def finish(i):
            for w in range(2):
                t_copy(i, w, 1, partner, 1).wait()
                t_copy(i, w, 1, y, 0).wait_send()
                t_copy(i, w, 0, partner, 1).wait_recv()

        loop(0, tiles, finish)


def run_ranks(hits, gates, tokens, cotangent, w_gate, w_up, w_down):
    all_slots, width = hits.shape[1], tokens.shape[1]
    rows, hid = w_gate.shape[1:]
    experts = all_slots // rows
    half, hid_blocks, all_rows = width // 2, hid // rows, 2 * PLANE * rows
    tiles = half // TILE
    bf16, f32, vmem, dma = jnp.bfloat16, jnp.float32, pltpu.VMEM, pltpu.SemaphoreType.DMA
    grad = jax.ShapeDtypeStruct((width // rows, rows, hid), bf16)
    in_vmem, anywhere = pl.BlockSpec(memory_space=vmem), pl.BlockSpec(memory_space=pl.ANY)
    return pl.pallas_call(
        rank_kernel,
        out_shape=(
            jax.ShapeDtypeStruct((experts, rows, width), bf16),
            grad,
            grad,
            jax.ShapeDtypeStruct((all_slots, width), bf16),
        ),
        in_specs=[in_vmem] * 4 + [anywhere] * 3,
        out_specs=[anywhere] * 3 + [in_vmem],
        scratch_shapes=[
            vmem((experts, rows, width), bf16),
            vmem((2, experts, rows, half), bf16),
            vmem((2, width // rows, rows, hid), bf16),
            vmem((2, width, hid), bf16),
            vmem((PLANE, rows, width), bf16),
            vmem((PLANE, 2, rows, width), bf16),
            vmem((all_rows, width), bf16),
            vmem((experts, 2, rows, half), bf16),
            vmem((PLANE, 2, rows, half), bf16),
            vmem((2, hid_blocks, rows, half), bf16),
            vmem((2 * hid, half), bf16),
            vmem((2, all_rows, hid), f32),
            vmem((2, all_rows, hid), bf16),
            vmem((2, all_rows, hid), bf16),
            vmem((all_rows, hid), f32),
            vmem((all_rows, 2 * hid), bf16),
            vmem((PLANE, 2, rows, half), bf16),
            vmem((PLANE, 2, rows, half), bf16),
            vmem((2, experts, rows, half), bf16),
            vmem((tiles, TILE, 2 * hid), bf16),
            vmem((tiles, TILE, 2 * hid), bf16),
            vmem((tiles, 2, TILE // rows, rows, hid), bf16),
            dma((2, HALF)),
            dma((2, NG // 2)),
            dma((2, 2, NG)),
            dma((2, 2)),
            dma((2, HALF)),
            dma((2, NG // 2)),
            dma((2, 3)),
            dma((2,)),
            dma((2, CHUNKS)),
            dma((2, 2 * CHUNKS)),
            dma((2, PLANE)),
            dma((2, 2, experts)),
            dma((2, tiles)),
            dma((2, 2, 2, tiles)),
        ],
        compiler_params=pltpu.CompilerParams(
            collective_id=0, has_side_effects=True, vmem_limit_bytes=54 << 20
        ),
    )(hits, gates, tokens, cotangent, w_gate, w_up, w_down)


def slot_tables(expert_ids, gate_values, flight_count, capacity):
    experts = jnp.arange(flight_count, dtype=jnp.int32)
    match = (expert_ids[:, :, None] == experts[None, None, :]).astype(jnp.float32)
    counted = jnp.sum(match, axis=1)
    before = jnp.cumsum(counted, axis=0) - counted
    places = jnp.arange(capacity, dtype=jnp.float32)
    slot_hit = counted[:, :, None] * (before[:, :, None] == places[None, None, :]).astype(
        jnp.float32
    )
    gate_each = jnp.sum(match * gate_values.astype(jnp.float32)[:, :, None], axis=1)
    return (match, slot_hit, gate_each)


def per_device(tokens, expert_ids, gate_values, cotangent, w_gate, w_up, w_down):
    device_count = lax.axis_size("expert")
    hidden_dev = w_gate.shape[1]
    slice_count = FFW // hidden_dev
    flight_count = device_count // slice_count
    width = tokens.shape[1]
    capacity = CAP
    f32, bf16 = jnp.float32, jnp.bfloat16
    match, slot_hit, gate_each = slot_tables(expert_ids, gate_values, flight_count, capacity)
    hit_flat = slot_hit.reshape(slot_hit.shape[0], flight_count * capacity).astype(bf16)
    gate_buf = jnp.sum(slot_hit * gate_each[:, :, None], axis=0).reshape(-1, 1)

    def to_blocks(weight):
        return weight.reshape(-1, capacity, weight.shape[1])

    returned, grad_gate, grad_up, cot_buf = run_ranks(
        hit_flat,
        gate_buf,
        tokens,
        cotangent,
        to_blocks(w_gate),
        to_blocks(w_up),
        to_blocks(w_down),
    )
    returned = returned.reshape(-1, width)
    weight_hit = (slot_hit * gate_each[:, :, None]).astype(bf16).reshape(hit_flat.shape)
    mixed = jnp.dot(weight_hit, returned, preferred_element_type=f32).astype(bf16)
    values = jnp.sum(returned.astype(f32) * cot_buf.astype(f32), axis=1).reshape(flight_count, capacity)
    value_each = jnp.einsum("tec,ec->te", slot_hit, values, precision=lax.Precision.HIGHEST)
    gate_grad = jnp.einsum("tke,te->tk", match, value_each, precision=lax.Precision.HIGHEST)
    grad_shape = (1, width, hidden_dev)
    return (mixed, gate_grad, grad_gate.reshape(grad_shape), grad_up.reshape(grad_shape))


def solution(mesh):
    placed = (
        P(("pipe", "expert"), None),
        P(("pipe", "expert"), None),
        P(("pipe", "expert"), None),
        P(("pipe", "expert"), None),
        P(None, "expert"),
        P(None, "expert"),
        P("expert", None),
    )
    return jax.shard_map(
        per_device,
        mesh=mesh,
        in_specs=placed,
        out_specs=(
            P(("pipe", "expert"), None),
            P(("pipe", "expert"), None),
            P("pipe", None, "expert"),
            P("pipe", None, "expert"),
        ),
        check_vma=False,
    )
```
